128 devices in a mesh: tok: 64 (over y, z_hi, x, core), head: 2 (over z_lo).
Axes of the slice: x: 4, y: 4, z: 4 (z_hi: 2, z_lo: 2; z = z_hi * 2 + z_lo), core: 2. Of those that a mesh axis runs over, the one named last changes fastest.
Arguments:
- inputs: bfloat16 [2, 32768, 2048], P(None, 'tok'), may hold values from -6 to 6
- projections: bfloat16 [3, 2048, 2048], P(None, None, 'head'), may hold values from -0.125 to 0.125
- lrate: float32 [2, 32768, 4], P(None, 'tok', 'head'), may hold values from 0.1 to 1
- fast_init: bfloat16 [4, 3, 384, 512], P('head'), may hold values from -0.25 to 0.25
- gain: float32 [2048], replicated, may hold values from 0.5 to 1.5
Outputs:
- normed: bfloat16 [2, 32768, 2048], P(None, ('tok', 'head'))
The draws below stay inside these ranges and needn't reach their ends.
All inputs are finite; a program needn't handle non-finite values.
Results may differ from the reference program's by a relative error of at most 0.018.
Values may be sent and summed in bfloat16 or wider, within the bound.
No kernel may reach another device: no remote copies, remote signals or barrier semaphores. Data moves between devices by JAX's collectives and lax.ppermute only.
A program may use at most 128 MiB of HBM per device.

```python
import math
import jax
import jax.numpy as jnp
from jax import lax

D = 2048
HEADS = 4
HD = 512
F = 384
INNER = 2
GROUPS = 2
TOKENS = 32768


def block_scale(key, shape, cuts, low, largest):
    factor_of, own = 1.0, jax.random.fold_in(key, 6)
    for position, shards_of in cuts:
        heights = jnp.exp(jax.random.uniform(jax.random.fold_in(own, position), (shards_of,), jnp.float32, low / len(cuts), largest / len(cuts)))
        factor_of = factor_of * jnp.repeat(heights, shape[position] // shards_of).reshape([-1 if axis == position else 1 for axis in range(len(shape))])
    return factor_of


def bell_draw(stream_key, shape, spread, most, pieces=(), kind=jnp.bfloat16):
    loudness = block_scale(stream_key, shape, pieces, -0.22, 0.18) if pieces else 1.0
    drawn = jax.random.normal(stream_key, shape, jnp.float32) * spread * loudness
    return jnp.minimum(jnp.maximum(drawn, -most), most).astype(kind)


def setup_inputs(seed: int = 0) -> dict:
    arg_keys = jax.random.split(jax.random.key(seed), 6)
    inputs = bell_draw(arg_keys[0], (GROUPS, TOKENS, D), 1.0, 6.0, ((1, 64),))
    projections = bell_draw(arg_keys[1], (3, D, D), D ** -0.5, 0.125, ((2, 2),))
    lrate = jnp.clip(jnp.exp(math.log(1.0) - 2.3025851 * jax.random.uniform(arg_keys[2], (GROUPS, TOKENS, HEADS), jnp.float32) ** block_scale(arg_keys[2], (GROUPS, TOKENS, HEADS), ((1, 64), (2, 2)), -0.2, 0.2)), 0.1, 1.0)
    fast_init = bell_draw(arg_keys[3], (HEADS, 3, F, HD), HD ** -0.5, 0.25, ((0, 2),))
    gain = jnp.clip(1.0 + 0.1 * jax.random.normal(arg_keys[4], (D,), jnp.float32), 0.5, 1.5)
    return dict(inputs=inputs, projections=projections, lrate=lrate, fast_init=fast_init, gain=gain)


step_size = 4.0

def mult(form, left, right):
    return jnp.einsum(form, left.astype(jnp.float32), right.astype(jnp.float32))

def silu_parts(hidden):
    sigma = jax.nn.sigmoid(hidden)
    return (hidden * sigma, sigma * (1.0 + hidden * (1.0 - sigma)))

def token_gradients(weights, keys, values, rates):
    hidden = mult('htd,hfd->htf', keys, weights[:, 0])
    gated = mult('htd,hfd->htf', keys, weights[:, 1])
    act, slope = silu_parts(hidden)
    mixed = (act * gated).astype(jnp.bfloat16)
    signal = (-rates[:, :, None] * values.astype(jnp.float32)).astype(jnp.bfloat16)
    grad_second = mult('htf,htd->hfd', mixed, signal)
    back = mult('htd,hfd->htf', signal, weights[:, 2])
    grad_gate = (back * act).astype(jnp.bfloat16)
    grad_first = (back * gated * slope).astype(jnp.bfloat16)
    grad_one = mult('htf,htd->hfd', grad_first, keys)
    grad_three = mult('htf,htd->hfd', grad_gate, keys)
    return jnp.stack([grad_one, grad_three, grad_second], axis=1)

def refresh(weights, summed, target):
    frob = lax.optimization_barrier(jnp.sum(summed * summed, axis=(2, 3)))
    scale = step_size / jnp.sqrt(frob + 1e-06)
    update = weights.astype(jnp.float32) - scale[:, :, None, None] * summed
    length = jnp.sqrt(lax.optimization_barrier(jnp.sum(update * update, axis=-1, keepdims=True)) + 1e-06)
    return (update * (target / length)).astype(jnp.bfloat16)

def read_memory(weights, queries):
    hidden = mult('htd,hfd->htf', queries, weights[:, 0])
    gated = mult('htd,hfd->htf', queries, weights[:, 1])
    act, _ = silu_parts(hidden)
    mixed = (act * gated).astype(jnp.bfloat16)
    return mult('htf,hfd->htd', mixed, weights[:, 2]).astype(jnp.bfloat16)

def reference(inputs, projections, lrate, fast_init, gain):
    target = jnp.sqrt(lax.optimization_barrier(jnp.sum(jnp.square(fast_init.astype(jnp.float32)), axis=-1, keepdims=True)))
    weights = fast_init
    outputs = []
    for group in range(GROUPS):
        mapped = mult('td,sde->ste', inputs[group], projections).astype(jnp.bfloat16)
        split = mapped.reshape(3, TOKENS, HEADS, HD).transpose(0, 2, 1, 3)
        queries, keys, values = (split[0], split[1], split[2])
        rates = lrate[group].T
        for inner in range(INNER):
            summed = token_gradients(weights, keys, values, rates)
            weights = refresh(weights, summed, target)
        readout = read_memory(weights, queries)
        joined = readout.transpose(1, 0, 2).reshape(TOKENS, HEADS * HD).astype(jnp.float32)
        square_mean = lax.optimization_barrier(jnp.mean(joined * joined, axis=-1, keepdims=True))
        outputs.append((joined * lax.rsqrt(square_mean + 1e-06) * gain).astype(jnp.bfloat16))
    return jnp.stack(outputs)
```

```python
import functools

import jax
import jax.numpy as jnp
from jax import lax
from jax.experimental import pallas as pl
from jax.experimental.pallas import tpu as pltpu
from jax.sharding import Mesh
from jax.sharding import PartitionSpec as P

INNER = 2
STEP_SIZE = 4.0
EPS = 1e-06
TOK = ("tok_0", "tok_1", "tok_2", "tok_3")
CHIPS = ("tok_0", "tok_1", "tok_2")
PEERS = 32
HD = 512
F = 384
ROWS = 48
COLS = 128
SHARD = 3 * ROWS
NOTE = 16
CHUNK = 256
BF = jnp.bfloat16
F32 = jnp.float32
VMEM_LIMIT = 40 * 1024 * 1024


def params(**more):
    return pltpu.CompilerParams(vmem_limit_bytes=VMEM_LIMIT, **more)


def cost(flops, moved):
    return pl.CostEstimate(flops=int(flops), bytes_accessed=int(moved), transcendentals=0)


def nt(left, right):
    return lax.dot_general(left, right, (((1,), (1,)), ((), ())), preferred_element_type=F32)


def nn(left, right):
    return lax.dot_general(left, right, (((1,), (0,)), ((), ())), preferred_element_type=F32)


def keys_signals_kernel(ids, x_ref, w_ref, rate_ref, out_ref):
    step = pl.program_id(0)
    mapped = nn(x_ref[0], w_ref[0]).astype(BF)

    @pl.when(step < 2)
    def _():
        out_ref[...] = mapped

    @pl.when(step >= 2)
    def _():
        rates = jnp.where(ids[0] == 0, rate_ref[0, :, 0:1], rate_ref[0, :, 1:2])
        out_ref[...] = (-rates * mapped.astype(F32)).astype(BF)


def keys_signals(head, group, inputs, projections, lrate):
    tokens, width = inputs.shape[1:]
    return pl.pallas_call(
        keys_signals_kernel,
        out_shape=jax.ShapeDtypeStruct((tokens, 2 * HD), BF),
        grid_spec=pltpu.PrefetchScalarGridSpec(
            num_scalar_prefetch=1,
            grid=(4,),
            in_specs=[
                pl.BlockSpec((1, tokens, width), lambda j, ids: (group, 0, 0)),
                pl.BlockSpec((1, width, HD // 2), lambda j, ids: (1 + j // 2, 0, 2 * ids[0] + j % 2)),
                pl.BlockSpec((1, tokens, 2), lambda j, ids: (group, 0, 0)),
            ],
            out_specs=pl.BlockSpec((tokens, HD // 2), lambda j, ids: (0, j)),
        ),
        compiler_params=params(),
        cost_estimate=cost(4 * tokens * width * HD, 2 * tokens * width + 4 * width * HD),
    )(head, inputs, projections, lrate)


def queries_kernel(ids, x_ref, w_ref, out_ref):
    out_ref[...] = nn(x_ref[0], w_ref[0]).astype(BF)


def queries_of(head, group, inputs, projections):
    tokens, width = inputs.shape[1:]
    return pl.pallas_call(
        queries_kernel,
        out_shape=jax.ShapeDtypeStruct((tokens, HD), BF),
        grid_spec=pltpu.PrefetchScalarGridSpec(
            num_scalar_prefetch=1,
            grid=(2,),
            in_specs=[
                pl.BlockSpec((1, tokens, width), lambda j, ids: (group, 0, 0)),
                pl.BlockSpec((1, width, HD // 2), lambda j, ids: (0, 0, 2 * ids[0] + j)),
            ],
            out_specs=pl.BlockSpec((tokens, HD // 2), lambda j, ids: (0, j)),
        ),
        compiler_params=params(),
        cost_estimate=cost(2 * tokens * width * HD, 2 * tokens * width + 2 * width * HD),
    )(head, inputs, projections)


def gradients(w_ref, own_ref, other_ref, d_ref, out_ref):
    tokens = own_ref.shape[0]
    for place in range(0, 2 * tokens, CHUNK):
        source = own_ref if place < tokens else other_ref
        first = place % tokens
        keys = source[first : first + CHUNK, 0:HD]
        signals = source[first : first + CHUNK, HD : 2 * HD]
        hidden = nt(w_ref[0:F, :], keys)
        gated = nt(w_ref[F : 2 * F, :], keys)
        back = nt(w_ref[2 * F : 3 * F, :], signals)
        sigma = 0.5 * jnp.tanh(0.5 * hidden) + 0.5
        act = hidden * sigma
        d_ref[0:F, place : place + CHUNK] = (back * gated * (sigma + act * (1.0 - sigma))).astype(BF)
        d_ref[F : 2 * F, place : place + CHUNK] = (back * act).astype(BF)
        d_ref[2 * F : 3 * F, place : place + CHUNK] = (act * gated).astype(BF)
    for m in range(3):
        columns = slice(0, HD) if m < 2 else slice(HD, 2 * HD)
        grad = nn(d_ref[m * F : (m + 1) * F, 0:tokens], own_ref[:, columns])
        grad += nn(d_ref[m * F : (m + 1) * F, tokens : 2 * tokens], other_ref[:, columns])
        grad = grad.astype(BF)
        for r in range(F // ROWS):
            for c in range(HD // COLS):
                out_ref[r * (HD // COLS) + c, m * ROWS : (m + 1) * ROWS, :] = grad[
                    r * ROWS : (r + 1) * ROWS, c * COLS : (c + 1) * COLS
                ]


def renew(w_ref, shards_ref, target_ref, new_ref):
    notes = shards_ref[0, SHARD : SHARD + NOTE, :].astype(F32)
    for i in range(1, PEERS):
        notes += shards_ref[i, SHARD : SHARD + NOTE, :].astype(F32)
    for m in range(3):
        frob = notes[3 * m : 3 * m + 1, :] + notes[3 * m + 1 : 3 * m + 2, :] + notes[3 * m + 2 : 3 * m + 3, :]
        scale = STEP_SIZE * lax.rsqrt(frob + EPS)
        for r in range(F // ROWS):
            rows = slice(m * F + r * ROWS, m * F + (r + 1) * ROWS)
            updates = []
            total = None
            for c in range(HD // COLS):
                grad = shards_ref[r * (HD // COLS) + c, m * ROWS : (m + 1) * ROWS, :].astype(F32)
                update = w_ref[rows, c * COLS : (c + 1) * COLS].astype(F32) - scale * grad
                updates.append(update)
                total = update * update if total is None else total + update * update
            length = jnp.sum(total, axis=1, keepdims=True)
            factor = target_ref[rows, :] * lax.rsqrt(length + EPS)
            for c in range(HD // COLS):
                new_ref[rows, c * COLS : (c + 1) * COLS] = (updates[c] * factor).astype(BF)


def first_step_kernel(ids, init_ref, own_ref, other_ref, out_ref, w_ref, target_ref, d_ref):
    for m in range(3):
        rows = slice(m * F, (m + 1) * F)
        start = init_ref[0, m]
        w_ref[rows, :] = start
        start = start.astype(F32)
        length = jnp.sqrt(jnp.sum(start * start, axis=1, keepdims=True))
        target_ref[rows, :] = jnp.broadcast_to(length, (F, COLS))
    gradients(w_ref, own_ref, other_ref, d_ref, out_ref)


def next_step_kernel(old_ref, shards_ref, target_ref, own_ref, other_ref, out_ref, w_ref, d_ref):
    renew(old_ref, shards_ref, target_ref, w_ref)
    gradients(w_ref, own_ref, other_ref, d_ref, out_ref)


GRADS = jax.ShapeDtypeStruct((PEERS, SHARD, COLS), BF)
MEMORY = jax.ShapeDtypeStruct((3 * F, HD), BF)
TARGET = jax.ShapeDtypeStruct((3 * F, COLS), F32)


def first_step(core, fast_init, own, other):
    tokens = own.shape[0]
    whole = pl.BlockSpec((tokens, 2 * HD), lambda i, ids: (0, 0))
    return pl.pallas_call(
        first_step_kernel,
        out_shape=(GRADS, MEMORY, TARGET),
        grid_spec=pltpu.PrefetchScalarGridSpec(
            num_scalar_prefetch=1,
            grid=(1,),
            in_specs=[pl.BlockSpec((1, 3, F, HD), lambda i, ids: (ids[0], 0, 0, 0)), whole, whole],
            out_specs=(
                pl.BlockSpec(GRADS.shape, lambda i, ids: (0, 0, 0)),
                pl.BlockSpec(MEMORY.shape, lambda i, ids: (0, 0)),
                pl.BlockSpec(TARGET.shape, lambda i, ids: (0, 0)),
            ),
            scratch_shapes=[pltpu.VMEM((3 * F, 2 * tokens), BF)],
        ),
        compiler_params=params(),
        cost_estimate=cost(24 * tokens * F * HD, 8 << 20),
    )(core, fast_init, own, other)


def next_step(old, shards, target, own, other):
    tokens = own.shape[0]
    return pl.pallas_call(
        next_step_kernel,
        out_shape=(GRADS, MEMORY),
        scratch_shapes=[pltpu.VMEM((3 * F, 2 * tokens), BF)],
        compiler_params=params(),
        cost_estimate=cost(24 * tokens * F * HD, 8 << 20),
    )(old, shards, target, own, other)


def sum_kernel(parts_ref, out_ref):
    total = parts_ref[0].astype(F32)
    for i in range(1, PEERS):
        total += parts_ref[i].astype(F32)
    row = lax.broadcasted_iota(jnp.int32, (NOTE, COLS), 0)
    notes = jnp.zeros((NOTE, COLS), F32)
    for m in range(3):
        part = total[m * ROWS : (m + 1) * ROWS, :]
        left = jnp.broadcast_to(jnp.sum(part * part, keepdims=True), (NOTE, COLS))
        for piece in range(3):
            term = left.astype(BF).astype(F32)
            notes = jnp.where(row == 3 * m + piece, term, notes)
            left = left - term
    total = total.astype(BF)
    notes = notes.astype(BF)
    for i in range(PEERS):
        out_ref[i, 0:SHARD, :] = total
        out_ref[i, SHARD : SHARD + NOTE, :] = notes


def sum_shards(parts):
    return pl.pallas_call(
        sum_kernel,
        out_shape=jax.ShapeDtypeStruct((PEERS, SHARD + NOTE, COLS), BF),
        compiler_params=params(),
        cost_estimate=cost(2 * parts.size, 4 * parts.size),
    )(parts)


def exchange(x):
    return lax.all_to_all(x, CHIPS, 0, 0, tiled=True)


def read(w_ref, queries):
    hidden = nt(queries, w_ref[0:F, :])
    gated = nt(queries, w_ref[F : 2 * F, :])
    sigma = 0.5 * jnp.tanh(0.5 * hidden) + 0.5
    mixed = (hidden * sigma * gated).astype(BF)
    return nn(mixed, w_ref[2 * F : 3 * F, :]).astype(BF)


def read_kernel(ids, w_ref, own_ref, other_ref, own_out, other_out):
    own_out[...] = read(w_ref, own_ref[...])
    other_out[...] = read(w_ref, other_ref[...])


def renew_read_kernel(ids, old_ref, shards_ref, target_ref, own_ref, other_ref, own_out, other_out, w_ref):
    renew(old_ref, shards_ref, target_ref, w_ref)
    own_out[...] = read(w_ref, own_ref[...])
    other_out[...] = read(w_ref, other_ref[...])


def read_half(half, memory, own, other):
    tokens = own.shape[0] // 2
    part = pl.BlockSpec((tokens, HD), lambda i, ids: (ids[0], 0))
    back = pl.BlockSpec((tokens, HD), lambda i, ids: (0, 0))
    out = jax.ShapeDtypeStruct((tokens, HD), BF)
    fixed = [pl.BlockSpec(x.shape, lambda i, ids, n=x.ndim: (0,) * n) for x in memory]
    renewed = len(memory) > 1
    return pl.pallas_call(
        renew_read_kernel if renewed else read_kernel,
        out_shape=(out, out, MEMORY) if renewed else (out, out),
        grid_spec=pltpu.PrefetchScalarGridSpec(
            num_scalar_prefetch=1,
            grid=(1,),
            in_specs=[*fixed, part, part],
            out_specs=(back, back, pl.BlockSpec(MEMORY.shape, lambda i, ids: (0, 0))) if renewed else (back, back),
        ),
        compiler_params=params(),
        cost_estimate=cost(12 * tokens * F * HD, 4 << 20),
    )(half, *memory, own, other)


def norm_kernel(ids, a_ref, b_ref, c_ref, d_ref, gain_ref, *rest):
    out_ref = rest[-1]
    core, far = ids[0], ids[1]
    pieces = (a_ref, b_ref, c_ref, d_ref)
    heads = (2 * far + core, 2 * far + 1 - core, 2 * (1 - far) + core, 2 * (1 - far) + 1 - core)
    total = None
    for piece in pieces:
        value = piece[...].astype(F32)
        square = jnp.sum(value * value, axis=1, keepdims=True)
        total = square if total is None else total + square
    scale = lax.rsqrt(total / (4 * HD) + EPS)
    for piece, head in zip(pieces, heads):
        columns = pl.ds(pl.multiple_of(head * HD, HD), HD)
        out_ref[0, :, columns] = (piece[...].astype(F32) * scale * gain_ref[0:1, columns]).astype(BF)


def normalise(ids, group, groups, pieces, gain, former):
    tokens = pieces[0].shape[0]
    part = pl.BlockSpec((tokens, HD), lambda i, ids: (0, 0))
    more = [] if former is None else [former]
    return pl.pallas_call(
        norm_kernel,
        out_shape=jax.ShapeDtypeStruct((groups, tokens, 4 * HD), BF),
        grid_spec=pltpu.PrefetchScalarGridSpec(
            num_scalar_prefetch=1,
            grid=(1,),
            in_specs=[part] * 4
            + [pl.BlockSpec((1, 4 * HD), lambda i, ids: (0, 0))]
            + [pl.BlockSpec(memory_space=pl.ANY)] * len(more),
            out_specs=pl.BlockSpec((1, tokens, 4 * HD), lambda i, ids: (group, 0, 0)),
        ),
        input_output_aliases={} if former is None else {6: 0},
        compiler_params=params(),
        cost_estimate=cost(8 * tokens * HD * 4, 4 * tokens * HD * 4),
    )(ids, *pieces, gain, *more)


def body(inputs, projections, lrate, fast_init, gain):
    groups = inputs.shape[0]
    core = lax.axis_index("tok_3").astype(jnp.int32)
    far = lax.axis_index("head").astype(jnp.int32)
    mine = core.reshape(1)
    mates = (1 - core).reshape(1)
    near_half = far.reshape(1)
    far_half = (1 - far).reshape(1)
    ids = jnp.stack([core, far])
    gain = gain.reshape(1, -1)
    swap = [(0, 1), (1, 0)]
    both = [(0, 3), (1, 2), (2, 1), (3, 0)]

    def swapped(x):
        return lax.ppermute(x, "tok_3", swap)

    def pairs(group, dep=None):
        x, w = inputs, projections
        start, later = mates, mine
        if dep is not None:
            start, later, _ = lax.optimization_barrier((mates, mine, dep))
        other = swapped(keys_signals(start, group, x, w, lrate))
        own = keys_signals(later, group, x, w, lrate)
        return own, other

    def asks(group, dep):
        start, later, _ = lax.optimization_barrier((mates, mine, dep))
        other = swapped(queries_of(start, group, inputs, projections))
        own = queries_of(later, group, inputs, projections)
        return own, other

    def finish(group, far_parts, near_parts, former):
        ahead = lax.ppermute(far_parts[0], "head", swap)
        across = lax.ppermute(far_parts[1], ("tok_3", "head"), both)
        beside = swapped(near_parts[1])
        return normalise(ids, group, groups, (near_parts[0], beside, ahead, across), gain, former)

    result = None
    pair = pairs(0)
    grads, memory, target = first_step(mine, fast_init, *pair)
    asked = None
    for group in range(groups):
        for inner in range(INNER):
            if inner == 0:
                asked = asks(group, grads)
            elif group + 1 < groups:
                later_pair = pairs(group + 1, grads)
            shards = exchange(sum_shards(exchange(grads)))
            if inner + 1 < INNER:
                grads, memory = next_step(memory, shards, target, *pair)
            elif group + 1 < groups:
                pair = later_pair
                grads, memory = next_step(memory, shards, target, *pair)
                far_parts = read_half(far_half, (memory,), *asked)
                near_parts = read_half(near_half, (memory,), *asked)
                result = finish(group, far_parts, near_parts, result)
            else:
                *far_parts, memory = read_half(far_half, (memory, shards, target), *asked)
                near_parts = read_half(near_half, (memory,), *asked)
                result = finish(group, far_parts, near_parts, result)
    return result


def solution(mesh):
    finer = Mesh(
        mesh.devices.reshape(4, 2, 4, 2, mesh.shape["head"]),
        ("tok_0", "tok_1", "tok_2", "tok_3", "head"),
    )
    placed = (
        P(None, TOK, None),
        P(None, None, "head"),
        P(None, TOK, "head"),
        P("head", None, None, None),
        P(),
    )
    return jax.shard_map(
        body, mesh=finer, in_specs=placed, out_specs=P(None, (*TOK, "head"), None), check_vma=False
    )
```

```python
import functools

import jax
import jax.numpy as jnp
from jax import lax
from jax.experimental import pallas as pl
from jax.experimental.pallas import tpu as pltpu
from jax.sharding import Mesh
from jax.sharding import PartitionSpec as P

STEP_SIZE = 4.0
EPS = 1e-06
TOK = ("y", "z_hi", "x", "core")
PLANE = ("y", "x")
PEERS = 16
HD = 512
F = 192
ROWS = 48
COLS = 128
SHARD = 3 * ROWS
NOTE = 16
CHUNK = 256
DEPTHS = 4
AHEAD = 8
BF = jnp.bfloat16
F32 = jnp.float32
MIB = 1024 * 1024


def params(limit=24):
    return pltpu.CompilerParams(vmem_limit_bytes=limit * MIB)


def cost(flops, moved):
    return pl.CostEstimate(flops=int(flops), bytes_accessed=int(moved), transcendentals=0)


def nt(left, right):
    return lax.dot_general(left, right, (((1,), (1,)), ((), ())), preferred_element_type=F32)


def nn(left, right):
    return lax.dot_general(left, right, (((1,), (0,)), ((), ())), preferred_element_type=F32)


def project_kernel(jobs, ids, x_ref, w_ref, rate_ref, *rest):
    *outs, x_buf, w_buf, x_sem, w_sem = rest
    groups = sorted({group for group, _ in jobs})
    kinds = sorted({kind for _, kind in jobs})
    depth = x_buf.shape[2] // DEPTHS
    half = x_buf.shape[1] // 2
    columns = pl.ds(pl.multiple_of(ids[0] * HD, HD), HD)
    copies = []
    for k in range(DEPTHS):
        part = pl.ds(k * depth, depth)
        some = []
        for g, group in enumerate(groups):
            for h, place in enumerate((ids[1], 1 - ids[1])):
                source = x_ref.at[group, pl.ds(pl.multiple_of(place * half, half), half), part]
                target = x_buf.at[g, pl.ds(h * half, half), part]
                some.append(pltpu.make_async_copy(source, target, x_sem.at[g, h, k]))
        for m, kind in enumerate(kinds):
            source = w_ref.at[kind, part, columns]
            some.append(pltpu.make_async_copy(source, w_buf.at[m, part, :], w_sem.at[m, k]))
        for copy in some:
            copy.start()
        copies.append(some)
    totals = [None] * len(jobs)
    for k in range(DEPTHS):
        for copy in copies[k]:
            copy.wait()
        part = slice(k * depth, (k + 1) * depth)
        for n, (group, kind) in enumerate(jobs):
            term = nn(x_buf[groups.index(group), :, part], w_buf[kinds.index(kind), part, :])
            totals[n] = term if k == 0 else totals[n] + term
    for n, (group, kind) in enumerate(jobs):
        result = totals[n].astype(BF)
        if kind == 2:
            rates = jnp.where(ids[0] == 0, rate_ref[group, 0:1, :], rate_ref[group, 1:2, :])
            low, high = rates[:, 0:half], rates[:, half : 2 * half]
            rates = jnp.concatenate(
                [jnp.where(ids[1] == 0, low, high), jnp.where(ids[1] == 0, high, low)], axis=1
            )
            rates = jnp.transpose(jnp.broadcast_to(rates, (8, 2 * half)))[:, 0:1]
            result = (-rates * result.astype(F32)).astype(BF)
        outs[n // 2][:, n % 2 * HD : (n % 2 + 1) * HD] = result


def project(ids, jobs, inputs, projections, rates):
    tokens, width = inputs.shape[1:]
    groups = len({group for group, _ in jobs})
    kinds = len({kind for _, kind in jobs})
    count = len(jobs)
    return pl.pallas_call(
        functools.partial(project_kernel, jobs),
        out_shape=[jax.ShapeDtypeStruct((tokens, 2 * HD), BF)] * (count // 2),
        grid_spec=pltpu.PrefetchScalarGridSpec(
            num_scalar_prefetch=1,
            grid=(1,),
            in_specs=[
                pl.BlockSpec(memory_space=pltpu.HBM),
                pl.BlockSpec(memory_space=pltpu.HBM),
                pl.BlockSpec(rates.shape, lambda i, ids: (0, 0, 0)),
            ],
            out_specs=[pl.BlockSpec((tokens, 2 * HD), lambda i, ids: (0, 0))] * (count // 2),
            scratch_shapes=[
                pltpu.VMEM((groups, tokens, width), BF),
                pltpu.VMEM((kinds, width, HD), BF),
                pltpu.SemaphoreType.DMA((groups, 2, DEPTHS)),
                pltpu.SemaphoreType.DMA((kinds, DEPTHS)),
            ],
        ),
        compiler_params=params(46),
        cost_estimate=cost(2 * count * tokens * width * HD, 2 * groups * tokens * width + 2 * kinds * width * HD),
    )(ids, inputs, projections, rates)


def fetches(pieces, ks_buf, sem):
    copies = []
    for piece in pieces:
        for first in range(0, piece.shape[0], CHUNK):
            n = len(copies)
            source = piece.at[pl.ds(first, CHUNK), pl.ds(0, 2 * HD)]
            copies.append(pltpu.make_async_copy(source, ks_buf.at[pl.ds(n * CHUNK, CHUNK), :], sem.at[n]))
    for copy in copies[:AHEAD]:
        copy.start()
    return copies


def gradients(w_ref, copies, ks_buf, d_ref, out_ref):
    for n, copy in enumerate(copies):
        copy.wait()
        if n + AHEAD < len(copies):
            copies[n + AHEAD].start()
        some = slice(n * CHUNK, (n + 1) * CHUNK)
        both = nt(w_ref[0 : 2 * F, :], ks_buf[some, 0:HD])
        back = nt(w_ref[2 * F : 3 * F, :], ks_buf[some, HD : 2 * HD])
        hidden, gated = both[0:F, :], both[F : 2 * F, :]
        sigma = 0.5 * jnp.tanh(0.5 * hidden) + 0.5
        act = hidden * sigma
        d_ref[0:F, some] = (back * gated * (sigma + act * (1.0 - sigma))).astype(BF)
        d_ref[F : 2 * F, some] = (back * act).astype(BF)
        d_ref[2 * F : 3 * F, some] = (act * gated).astype(BF)
    grads = [nn(d_ref[0 : 2 * F, :], ks_buf[:, 0:HD]).astype(BF)]
    grads.append(nn(d_ref[2 * F : 3 * F, :], ks_buf[:, HD : 2 * HD]).astype(BF))
    for m in range(3):
        for r in range(F // ROWS):
            first = (m % 2) * F * (m < 2) + r * ROWS
            for c in range(HD // COLS):
                out_ref[r * (HD // COLS) + c, m * ROWS : (m + 1) * ROWS, :] = grads[m // 2][
                    first : first + ROWS, c * COLS : (c + 1) * COLS
                ]


def renew(w_ref, shards_ref, target_ref, new_ref):
    notes = shards_ref[0, SHARD : SHARD + NOTE, :].astype(F32)
    for i in range(1, PEERS):
        notes += shards_ref[i, SHARD : SHARD + NOTE, :].astype(F32)
    for m in range(3):
        frob = notes[3 * m : 3 * m + 1, :] + notes[3 * m + 1 : 3 * m + 2, :] + notes[3 * m + 2 : 3 * m + 3, :]
        scale = STEP_SIZE * lax.rsqrt(frob + EPS)
        for r in range(F // ROWS):
            rows = slice(m * F + r * ROWS, m * F + (r + 1) * ROWS)
            updates = []
            total = None
            for c in range(HD // COLS):
                grad = shards_ref[r * (HD // COLS) + c, m * ROWS : (m + 1) * ROWS, :].astype(F32)
                update = w_ref[rows, c * COLS : (c + 1) * COLS].astype(F32) - scale * grad
                updates.append(update)
                total = update * update if total is None else total + update * update
            length = jnp.sum(total, axis=1, keepdims=True)
            factor = target_ref[rows, :] * lax.rsqrt(length + EPS)
            for c in range(HD // COLS):
                new_ref[rows, c * COLS : (c + 1) * COLS] = (updates[c] * factor).astype(BF)


def start_kernel(ids, init_ref, w_ref, target_ref):
    for m in range(3):
        rows = slice(m * F, (m + 1) * F)
        start = init_ref[0, m]
        w_ref[rows, :] = start
        start = start.astype(F32)
        length = jnp.sqrt(jnp.sum(start * start, axis=1, keepdims=True))
        target_ref[rows, :] = jnp.broadcast_to(length, (F, COLS))


def first_step_kernel(w_ref, *rest):
    *pieces, out_ref, ks_buf, d_ref, sem = rest
    copies = fetches(pieces, ks_buf, sem)
    gradients(w_ref, copies, ks_buf, d_ref, out_ref)


def next_step_kernel(old_ref, shards_ref, target_ref, *rest):
    *pieces, out_ref, w_ref, ks_buf, d_ref, sem = rest
    copies = fetches(pieces, ks_buf, sem)
    renew(old_ref, shards_ref, target_ref, w_ref)
    gradients(w_ref, copies, ks_buf, d_ref, out_ref)


def renew_kernel(old_ref, shards_ref, target_ref, w_ref):
    renew(old_ref, shards_ref, target_ref, w_ref)


GRADS = jax.ShapeDtypeStruct((PEERS, SHARD, COLS), BF)
MEMORY = jax.ShapeDtypeStruct((3 * F, HD), BF)
TARGET = jax.ShapeDtypeStruct((3 * F, COLS), F32)
SQUARES = jax.ShapeDtypeStruct((8, COLS), F32)


def step_scratch(pieces):
    tokens = sum(piece.shape[0] for piece in pieces)
    return [
        pltpu.VMEM((tokens, 2 * HD), BF),
        pltpu.VMEM((3 * F, tokens), BF),
        pltpu.SemaphoreType.DMA((tokens // CHUNK,)),
    ]


def step_cost(pieces):
    tokens = sum(piece.shape[0] for piece in pieces)
    return cost(12 * tokens * F * HD, 8 << 20)


def start_memory(ids, fast_init):
    return pl.pallas_call(
        start_kernel,
        out_shape=(MEMORY, TARGET),
        grid_spec=pltpu.PrefetchScalarGridSpec(
            num_scalar_prefetch=1,
            grid=(1,),
            in_specs=[pl.BlockSpec((1, 3, F, HD), lambda i, ids: (ids[0], 0, ids[1], 0))],
            out_specs=(
                pl.BlockSpec(MEMORY.shape, lambda i, ids: (0, 0)),
                pl.BlockSpec(TARGET.shape, lambda i, ids: (0, 0)),
            ),
        ),
        compiler_params=params(),
        cost_estimate=cost(9 * F * HD, 4 << 20),
    )(ids, fast_init)


def first_step(memory, pieces):
    whole = pl.BlockSpec(memory_space=pltpu.VMEM)
    return pl.pallas_call(
        first_step_kernel,
        out_shape=GRADS,
        in_specs=[whole] + [pl.BlockSpec(memory_space=pltpu.HBM)] * len(pieces),
        out_specs=whole,
        scratch_shapes=step_scratch(pieces),
        compiler_params=params(),
        cost_estimate=step_cost(pieces),
    )(memory, *pieces)


def next_step(old, shards, target, pieces):
    whole = pl.BlockSpec(memory_space=pltpu.VMEM)
    return pl.pallas_call(
        next_step_kernel,
        out_shape=(GRADS, MEMORY),
        in_specs=[whole] * 3 + [pl.BlockSpec(memory_space=pltpu.HBM)] * len(pieces),
        out_specs=(whole, whole),
        scratch_shapes=step_scratch(pieces),
        compiler_params=params(),
        cost_estimate=step_cost(pieces),
    )(old, shards, target, *pieces)


def last_memory(old, shards, target):
    return pl.pallas_call(
        renew_kernel,
        out_shape=MEMORY,
        compiler_params=params(),
        cost_estimate=cost(8 * old.size, 6 * old.size),
    )(old, shards, target)


def sum_kernel(parts_ref, out_ref, squares_ref):
    total = parts_ref[0].astype(F32)
    for i in range(1, PEERS):
        total += parts_ref[i].astype(F32)
    out_ref[...] = total.astype(BF)
    row = lax.broadcasted_iota(jnp.int32, SQUARES.shape, 0)
    squares = jnp.zeros(SQUARES.shape, F32)
    for m in range(3):
        part = total[m * ROWS : (m + 1) * ROWS, :]
        squares = jnp.where(row == m, jnp.sum(part * part, keepdims=True), squares)
    squares_ref[...] = squares


def sum_shards(parts):
    return pl.pallas_call(
        sum_kernel,
        out_shape=(jax.ShapeDtypeStruct((SHARD, COLS), BF), SQUARES),
        compiler_params=params(),
        cost_estimate=cost(2 * parts.size, 2 * parts.size),
    )(parts)


def note_kernel(shard_ref, here_ref, there_ref, out_ref):
    squares = here_ref[...] + there_ref[...]
    row = lax.broadcasted_iota(jnp.int32, (NOTE, COLS), 0)
    notes = jnp.zeros((NOTE, COLS), F32)
    for m in range(3):
        left = jnp.broadcast_to(squares[m : m + 1, :], (NOTE, COLS))
        for piece in range(3):
            term = left.astype(BF).astype(F32)
            notes = jnp.where(row == 3 * m + piece, term, notes)
            left = left - term
    notes = notes.astype(BF)
    shard = shard_ref[...]
    for i in range(PEERS):
        out_ref[i, 0:SHARD, :] = shard
        out_ref[i, SHARD : SHARD + NOTE, :] = notes


def with_notes(shard, here, there):
    return pl.pallas_call(
        note_kernel,
        out_shape=jax.ShapeDtypeStruct((PEERS, SHARD + NOTE, COLS), BF),
        compiler_params=params(),
        cost_estimate=cost(4 * shard.size, 2 * PEERS * shard.size),
    )(shard, here, there)


def exchange(x, beside):
    moved = lax.all_to_all(x, PLANE, 0, 0, tiled=True)
    if beside is None:
        return moved, None
    return lax.optimization_barrier((moved, beside(x)))


def read_kernel(here_ref, there_ref, *rest):
    count = len(rest) // 2
    for queries_ref, out_ref in zip(rest[:count], rest[count:]):
        queries = queries_ref[...]
        total = None
        for w_ref in (here_ref, there_ref):
            hidden = nt(queries, w_ref[0:F, :])
            gated = nt(queries, w_ref[F : 2 * F, :])
            sigma = 0.5 * jnp.tanh(0.5 * hidden) + 0.5
            mixed = (hidden * sigma * gated).astype(BF)
            term = nn(mixed, w_ref[2 * F : 3 * F, :])
            total = term if total is None else total + term
        out_ref[...] = total.astype(BF)


def read(half, here, there, own, own_place, foreign, foreign_place):
    tokens = own.shape[0] // 2
    memory = pl.BlockSpec(MEMORY.shape, lambda i: (0, 0))
    back = pl.BlockSpec((tokens, HD), lambda i: (0, 0))
    out = jax.ShapeDtypeStruct((tokens, HD), BF)
    return pl.pallas_call(
        read_kernel,
        out_shape=(out, out),
        grid=(1,),
        in_specs=[
            memory,
            memory,
            pl.BlockSpec((tokens, HD), lambda i: (half, own_place)),
            pl.BlockSpec((tokens, HD), lambda i: (half, foreign_place)),
        ],
        out_specs=(back, back),
        compiler_params=params(),
        cost_estimate=cost(24 * tokens * F * HD, 4 << 20),
    )(here, there, own, foreign)


def norm_kernel(ids, a_ref, b_ref, c_ref, d_ref, gain_ref, *rest):
    out_ref = rest[-1]
    head, far = ids[0], ids[1]
    pieces = (a_ref, b_ref, c_ref, d_ref)
    heads = (2 * far + head, 2 * far + 1 - head, 2 * (1 - far) + head, 2 * (1 - far) + 1 - head)
    total = None
    for piece in pieces:
        value = piece[...].astype(F32)
        square = jnp.sum(value * value, axis=1, keepdims=True)
        total = square if total is None else total + square
    scale = lax.rsqrt(total / (4 * HD) + EPS)
    for piece, place in zip(pieces, heads):
        columns = pl.ds(pl.multiple_of(place * HD, HD), HD)
        out_ref[0, :, columns] = (piece[...].astype(F32) * scale * gain_ref[0:1, columns]).astype(BF)


def normalise(ids, group, groups, pieces, gain, former):
    tokens = pieces[0].shape[0]
    part = pl.BlockSpec((tokens, HD), lambda i, ids: (0, 0))
    more = [] if former is None else [former]
    return pl.pallas_call(
        norm_kernel,
        out_shape=jax.ShapeDtypeStruct((groups, tokens, 4 * HD), BF),
        grid_spec=pltpu.PrefetchScalarGridSpec(
            num_scalar_prefetch=1,
            grid=(1,),
            in_specs=[part] * 4
            + [pl.BlockSpec((1, 4 * HD), lambda i, ids: (0, 0))]
            + [pl.BlockSpec(memory_space=pl.ANY)] * len(more),
            out_specs=pl.BlockSpec((1, tokens, 4 * HD), lambda i, ids: (group, 0, 0)),
        ),
        input_output_aliases={} if former is None else {6: 0},
        compiler_params=params(),
        cost_estimate=cost(8 * tokens * HD * 4, 4 * tokens * HD * 4),
    )(ids, *pieces, gain, *more)


SWAP = [(0, 1), (1, 0)]
BOTH = [(0, 3), (1, 2), (2, 1), (3, 0)]


def body(inputs, projections, lrate, fast_init, gain):
    groups = inputs.shape[0]
    plane = lax.axis_index("z_hi").astype(jnp.int32)
    core = lax.axis_index("core").astype(jnp.int32)
    far = lax.axis_index("head").astype(jnp.int32)
    kept = jnp.stack([plane, far])
    given = jnp.stack([1 - plane, far])
    share = jnp.stack([plane, core])
    gain = gain.reshape(1, -1)
    rates = lrate.transpose(0, 2, 1)

    def across(x):
        return lax.ppermute(x, "core", SWAP)

    def beyond(x):
        return lax.ppermute(x, "z_hi", SWAP)

    def after(ids, dep):
        return ids if dep is None else lax.optimization_barrier((ids, dep))[0]

    def of(ids, jobs, dep=None):
        return project(after(ids, dep), jobs, inputs, projections, rates)

    def to_rows(far_parts, near_parts):
        ahead = lax.ppermute(far_parts[0], "head", SWAP)
        askew = lax.ppermute(far_parts[1], ("z_hi", "head"), BOTH)
        return near_parts[0], beyond(near_parts[1]), ahead, askew

    def summed(grads, beside_sum=None, beside_gather=None):
        parts, first = exchange(grads, beside_sum)
        shard, squares = sum_shards(parts)
        shards, second = exchange(with_notes(shard, squares, across(squares)), beside_gather)
        return shards, first, second

    def readouts(memory, *asked):
        mate = across(memory)
        return read(1, memory, mate, *asked), read(0, memory, mate, *asked)

    later = ((1, 1), (1, 2), (1, 0), (0, 0))
    (given_now,) = of(given, ((0, 1), (0, 2)))
    foreign = beyond(given_now)
    (own,) = of(kept, ((0, 1), (0, 2)))
    own_mate = across(own)
    given_next, given_asked = of(given, later, own)
    memory, target = start_memory(after(share, given_next), fast_init)
    foreign, memory, given_next, given_asked = lax.optimization_barrier((foreign, memory, given_next, given_asked))
    foreign_next = beyond(given_next)
    foreign_asked = beyond(given_asked)
    pieces = (own, own_mate, foreign, across(foreign))
    grads = first_step(memory, pieces)
    shards, (own_next, own_asked), _ = summed(grads, lambda dep: tuple(of(kept, later, dep)))
    grads, memory = next_step(memory, shards, target, pieces)
    shards, (foreign_next, own_next_mate), (foreign_next_mate, foreign_asked) = summed(
        grads,
        lambda dep: (foreign_next, across(own_next)),
        lambda dep: (across(foreign_next), foreign_asked),
    )
    pieces = (own_next, own_next_mate, foreign_next, foreign_next_mate)

    grads, memory = next_step(memory, shards, target, pieces)
    parts = readouts(memory, own_asked, 1, foreign_asked, 1)
    grads, parts = lax.optimization_barrier((grads, parts))
    shards, _, _ = summed(grads)
    rows_then = to_rows(*parts)
    grads, memory = next_step(memory, shards, target, pieces)
    shards, _, rows_then = summed(grads, None, lambda dep: rows_then)
    memory = last_memory(memory, shards, target)
    rows = to_rows(*readouts(memory, own_asked, 0, foreign_asked, 0))
    result = normalise(after(kept, memory), 0, groups, rows_then, gain, None)
    return normalise(kept, 1, groups, rows, gain, result)


def solution(mesh):
    finer = Mesh(
        mesh.devices.reshape(4, 2, 4, 2, mesh.shape["head"]),
        (*TOK, "head"),
    )
    placed = (
        P(None, TOK, None),
        P(None, None, "head"),
        P(None, TOK, "head"),
        P("head", None, None, None),
        P(),
    )
    return jax.shard_map(
        body, mesh=finer, in_specs=placed, out_specs=P(None, (*TOK, "head"), None), check_vma=False
    )
```

```python
import functools

import jax
import jax.numpy as jnp
from jax import lax
from jax.experimental import pallas as pl
from jax.experimental.pallas import tpu as pltpu
from jax.sharding import Mesh
from jax.sharding import PartitionSpec as P

STEP_SIZE = 4.0
EPS = 1e-06
TOK = ("y", "z_hi", "x", "core")
PLANE = ("y", "x")
PEERS = 16
HD = 512
F = 192
ROWS = 48
COLS = 128
SHARD = 3 * ROWS
NOTE = 16
CHUNK = 256
DEPTHS = 4
AHEAD = 8
BF = jnp.bfloat16
F32 = jnp.float32
MIB = 1024 * 1024


def params(limit=24):
    return pltpu.CompilerParams(vmem_limit_bytes=limit * MIB)


def cost(flops, moved):
    return pl.CostEstimate(flops=int(flops), bytes_accessed=int(moved), transcendentals=0)


def nt(left, right):
    return lax.dot_general(left, right, (((1,), (1,)), ((), ())), preferred_element_type=F32)


def nn(left, right):
    return lax.dot_general(left, right, (((1,), (0,)), ((), ())), preferred_element_type=F32)


def project_kernel(jobs, ids, x_ref, w_ref, rate_ref, *rest):
    *outs, x_buf, w_buf, x_sem, w_sem = rest
    groups = sorted({group for group, _ in jobs})
    kinds = sorted({kind for _, kind in jobs})
    depth = x_buf.shape[2] // DEPTHS
    half = x_buf.shape[1] // 2
    columns = pl.ds(pl.multiple_of(ids[0] * HD, HD), HD)
    copies = []
    for k in range(DEPTHS):
        part = pl.ds(k * depth, depth)
        some = []
        for g, group in enumerate(groups):
            for h, place in enumerate((ids[1], 1 - ids[1])):
                source = x_ref.at[group, pl.ds(pl.multiple_of(place * half, half), half), part]
                target = x_buf.at[g, pl.ds(h * half, half), part]
                some.append(pltpu.make_async_copy(source, target, x_sem.at[g, h, k]))
        for m, kind in enumerate(kinds):
            source = w_ref.at[kind, part, columns]
            some.append(pltpu.make_async_copy(source, w_buf.at[m, part, :], w_sem.at[m, k]))
        for copy in some:
            copy.start()
        copies.append(some)
    totals = [None] * len(jobs)
    for k in range(DEPTHS):
        for copy in copies[k]:
            copy.wait()
        part = slice(k * depth, (k + 1) * depth)
        for n, (group, kind) in enumerate(jobs):
            term = nn(x_buf[groups.index(group), :, part], w_buf[kinds.index(kind), part, :])
            totals[n] = term if k == 0 else totals[n] + term
    for n, (group, kind) in enumerate(jobs):
        result = totals[n].astype(BF)
        if kind == 2:
            rates = jnp.where(ids[0] == 0, rate_ref[group, 0:1, :], rate_ref[group, 1:2, :])
            low, high = rates[:, 0:half], rates[:, half : 2 * half]
            rates = jnp.concatenate(
                [jnp.where(ids[1] == 0, low, high), jnp.where(ids[1] == 0, high, low)], axis=1
            )
            rates = jnp.transpose(jnp.broadcast_to(rates, (8, 2 * half)))[:, 0:1]
            result = (-rates * result.astype(F32)).astype(BF)
        outs[n // 2][:, n % 2 * HD : (n % 2 + 1) * HD] = result


def project(ids, jobs, inputs, projections, rates):
    tokens, width = inputs.shape[1:]
    groups = len({group for group, _ in jobs})
    kinds = len({kind for _, kind in jobs})
    count = len(jobs)
    return pl.pallas_call(
        functools.partial(project_kernel, jobs),
        out_shape=[jax.ShapeDtypeStruct((tokens, 2 * HD), BF)] * (count // 2),
        grid_spec=pltpu.PrefetchScalarGridSpec(
            num_scalar_prefetch=1,
            grid=(1,),
            in_specs=[
                pl.BlockSpec(memory_space=pltpu.HBM),
                pl.BlockSpec(memory_space=pltpu.HBM),
                pl.BlockSpec(rates.shape, lambda i, ids: (0, 0, 0)),
            ],
            out_specs=[pl.BlockSpec((tokens, 2 * HD), lambda i, ids: (0, 0))] * (count // 2),
            scratch_shapes=[
                pltpu.VMEM((groups, tokens, width), BF),
                pltpu.VMEM((kinds, width, HD), BF),
                pltpu.SemaphoreType.DMA((groups, 2, DEPTHS)),
                pltpu.SemaphoreType.DMA((kinds, DEPTHS)),
            ],
        ),
        compiler_params=params(46),
        cost_estimate=cost(2 * count * tokens * width * HD, 2 * groups * tokens * width + 2 * kinds * width * HD),
    )(ids, inputs, projections, rates)


def fetches(pieces, ks_buf, sem):
    copies = []
    for piece in pieces:
        for first in range(0, piece.shape[0], CHUNK):
            n = len(copies)
            source = piece.at[pl.ds(first, CHUNK), pl.ds(0, 2 * HD)]
            copies.append(pltpu.make_async_copy(source, ks_buf.at[pl.ds(n * CHUNK, CHUNK), :], sem.at[n]))
    for copy in copies[:AHEAD]:
        copy.start()
    return copies


def gradients(w_ref, copies, ks_buf, d_ref, out_ref):
    for n, copy in enumerate(copies):
        copy.wait()
        if n + AHEAD < len(copies):
            copies[n + AHEAD].start()
        some = slice(n * CHUNK, (n + 1) * CHUNK)
        both = nt(w_ref[0 : 2 * F, :], ks_buf[some, 0:HD])
        back = nt(w_ref[2 * F : 3 * F, :], ks_buf[some, HD : 2 * HD])
        hidden, gated = both[0:F, :], both[F : 2 * F, :]
        sigma = 0.5 * jnp.tanh(0.5 * hidden) + 0.5
        act = hidden * sigma
        d_ref[0:F, some] = (back * gated * (sigma + act * (1.0 - sigma))).astype(BF)
        d_ref[F : 2 * F, some] = (back * act).astype(BF)
        d_ref[2 * F : 3 * F, some] = (act * gated).astype(BF)
    grads = [nn(d_ref[0 : 2 * F, :], ks_buf[:, 0:HD]).astype(BF)]
    grads.append(nn(d_ref[2 * F : 3 * F, :], ks_buf[:, HD : 2 * HD]).astype(BF))
    for m in range(3):
        for r in range(F // ROWS):
            first = (m % 2) * F * (m < 2) + r * ROWS
            for c in range(HD // COLS):
                out_ref[r * (HD // COLS) + c, m * ROWS : (m + 1) * ROWS, :] = grads[m // 2][
                    first : first + ROWS, c * COLS : (c + 1) * COLS
                ]


def renew(w_ref, shards_ref, target_ref, new_ref):
    notes = shards_ref[0, SHARD : SHARD + NOTE, :].astype(F32)
    for i in range(1, PEERS):
        notes += shards_ref[i, SHARD : SHARD + NOTE, :].astype(F32)
    for m in range(3):
        frob = notes[3 * m : 3 * m + 1, :] + notes[3 * m + 1 : 3 * m + 2, :] + notes[3 * m + 2 : 3 * m + 3, :]
        scale = STEP_SIZE * lax.rsqrt(frob + EPS)
        for r in range(F // ROWS):
            rows = slice(m * F + r * ROWS, m * F + (r + 1) * ROWS)
            updates = []
            total = None
            for c in range(HD // COLS):
                grad = shards_ref[r * (HD // COLS) + c, m * ROWS : (m + 1) * ROWS, :].astype(F32)
                update = w_ref[rows, c * COLS : (c + 1) * COLS].astype(F32) - scale * grad
                updates.append(update)
                total = update * update if total is None else total + update * update
            length = jnp.sum(total, axis=1, keepdims=True)
            factor = target_ref[rows, :] * lax.rsqrt(length + EPS)
            for c in range(HD // COLS):
                new_ref[rows, c * COLS : (c + 1) * COLS] = (updates[c] * factor).astype(BF)


def start_kernel(ids, init_ref, w_ref, target_ref):
    for m in range(3):
        rows = slice(m * F, (m + 1) * F)
        start = init_ref[0, m]
        w_ref[rows, :] = start
        start = start.astype(F32)
        length = jnp.sqrt(jnp.sum(start * start, axis=1, keepdims=True))
        target_ref[rows, :] = jnp.broadcast_to(length, (F, COLS))


def first_step_kernel(w_ref, *rest):
    *pieces, out_ref, ks_buf, d_ref, sem = rest
    copies = fetches(pieces, ks_buf, sem)
    gradients(w_ref, copies, ks_buf, d_ref, out_ref)


def next_step_kernel(old_ref, shards_ref, target_ref, *rest):
    *pieces, out_ref, w_ref, ks_buf, d_ref, sem = rest
    copies = fetches(pieces, ks_buf, sem)
    renew(old_ref, shards_ref, target_ref, w_ref)
    gradients(w_ref, copies, ks_buf, d_ref, out_ref)


def renew_kernel(old_ref, shards_ref, target_ref, w_ref):
    renew(old_ref, shards_ref, target_ref, w_ref)


GRADS = jax.ShapeDtypeStruct((PEERS, SHARD, COLS), BF)
MEMORY = jax.ShapeDtypeStruct((3 * F, HD), BF)
TARGET = jax.ShapeDtypeStruct((3 * F, COLS), F32)
SQUARES = jax.ShapeDtypeStruct((8, COLS), F32)


def step_scratch(pieces):
    tokens = sum(piece.shape[0] for piece in pieces)
    return [
        pltpu.VMEM((tokens, 2 * HD), BF),
        pltpu.VMEM((3 * F, tokens), BF),
        pltpu.SemaphoreType.DMA((tokens // CHUNK,)),
    ]


def step_cost(pieces):
    tokens = sum(piece.shape[0] for piece in pieces)
    return cost(12 * tokens * F * HD, 8 << 20)


def start_memory(ids, fast_init):
    return pl.pallas_call(
        start_kernel,
        out_shape=(MEMORY, TARGET),
        grid_spec=pltpu.PrefetchScalarGridSpec(
            num_scalar_prefetch=1,
            grid=(1,),
            in_specs=[pl.BlockSpec((1, 3, F, HD), lambda i, ids: (ids[0], 0, ids[1], 0))],
            out_specs=(
                pl.BlockSpec(MEMORY.shape, lambda i, ids: (0, 0)),
                pl.BlockSpec(TARGET.shape, lambda i, ids: (0, 0)),
            ),
        ),
        compiler_params=params(),
        cost_estimate=cost(9 * F * HD, 4 << 20),
    )(ids, fast_init)


def first_step(memory, pieces):
    whole = pl.BlockSpec(memory_space=pltpu.VMEM)
    return pl.pallas_call(
        first_step_kernel,
        out_shape=GRADS,
        in_specs=[whole] + [pl.BlockSpec(memory_space=pltpu.HBM)] * len(pieces),
        out_specs=whole,
        scratch_shapes=step_scratch(pieces),
        compiler_params=params(),
        cost_estimate=step_cost(pieces),
    )(memory, *pieces)


def next_step(old, shards, target, pieces):
    whole = pl.BlockSpec(memory_space=pltpu.VMEM)
    return pl.pallas_call(
        next_step_kernel,
        out_shape=(GRADS, MEMORY),
        in_specs=[whole] * 3 + [pl.BlockSpec(memory_space=pltpu.HBM)] * len(pieces),
        out_specs=(whole, whole),
        scratch_shapes=step_scratch(pieces),
        compiler_params=params(),
        cost_estimate=step_cost(pieces),
    )(old, shards, target, *pieces)


def last_memory(old, shards, target):
    return pl.pallas_call(
        renew_kernel,
        out_shape=MEMORY,
        compiler_params=params(),
        cost_estimate=cost(8 * old.size, 6 * old.size),
    )(old, shards, target)


def sum_kernel(parts_ref, out_ref, squares_ref):
    total = parts_ref[0].astype(F32)
    for i in range(1, PEERS):
        total += parts_ref[i].astype(F32)
    out_ref[...] = total.astype(BF)
    row = lax.broadcasted_iota(jnp.int32, SQUARES.shape, 0)
    squares = jnp.zeros(SQUARES.shape, F32)
    for m in range(3):
        part = total[m * ROWS : (m + 1) * ROWS, :]
        squares = jnp.where(row == m, jnp.sum(part * part, keepdims=True), squares)
    squares_ref[...] = squares


def sum_shards(parts):
    return pl.pallas_call(
        sum_kernel,
        out_shape=(jax.ShapeDtypeStruct((SHARD, COLS), BF), SQUARES),
        compiler_params=params(),
        cost_estimate=cost(2 * parts.size, 2 * parts.size),
    )(parts)


def note_kernel(shard_ref, here_ref, there_ref, out_ref):
    squares = here_ref[...] + there_ref[...]
    row = lax.broadcasted_iota(jnp.int32, (NOTE, COLS), 0)
    notes = jnp.zeros((NOTE, COLS), F32)
    for m in range(3):
        left = jnp.broadcast_to(squares[m : m + 1, :], (NOTE, COLS))
        for piece in range(3):
            term = left.astype(BF).astype(F32)
            notes = jnp.where(row == 3 * m + piece, term, notes)
            left = left - term
    notes = notes.astype(BF)
    shard = shard_ref[...]
    for i in range(PEERS):
        out_ref[i, 0:SHARD, :] = shard
        out_ref[i, SHARD : SHARD + NOTE, :] = notes


def with_notes(shard, here, there):
    return pl.pallas_call(
        note_kernel,
        out_shape=jax.ShapeDtypeStruct((PEERS, SHARD + NOTE, COLS), BF),
        compiler_params=params(),
        cost_estimate=cost(4 * shard.size, 2 * PEERS * shard.size),
    )(shard, here, there)


def exchange(x, beside):
    moved = lax.all_to_all(x, PLANE, 0, 0, tiled=True)
    if beside is None:
        return moved, None
    return lax.optimization_barrier((moved, beside(x)))


def read_kernel(here_ref, there_ref, *rest):
    count = len(rest) // 2
    for queries_ref, out_ref in zip(rest[:count], rest[count:]):
        queries = queries_ref[...]
        total = None
        for w_ref in (here_ref, there_ref):
            hidden = nt(queries, w_ref[0:F, :])
            gated = nt(queries, w_ref[F : 2 * F, :])
            sigma = 0.5 * jnp.tanh(0.5 * hidden) + 0.5
            mixed = (hidden * sigma * gated).astype(BF)
            term = nn(mixed, w_ref[2 * F : 3 * F, :])
            total = term if total is None else total + term
        out_ref[...] = total.astype(BF)


def read(half, here, there, own, own_place, foreign, foreign_place):
    tokens = own.shape[0] // 2
    memory = pl.BlockSpec(MEMORY.shape, lambda i: (0, 0))
    back = pl.BlockSpec((tokens, HD), lambda i: (0, 0))
    out = jax.ShapeDtypeStruct((tokens, HD), BF)
    return pl.pallas_call(
        read_kernel,
        out_shape=(out, out),
        grid=(1,),
        in_specs=[
            memory,
            memory,
            pl.BlockSpec((tokens, HD), lambda i: (half, own_place)),
            pl.BlockSpec((tokens, HD), lambda i: (half, foreign_place)),
        ],
        out_specs=(back, back),
        compiler_params=params(),
        cost_estimate=cost(24 * tokens * F * HD, 4 << 20),
    )(here, there, own, foreign)


def norm_kernel(ids, a_ref, b_ref, c_ref, d_ref, gain_ref, *rest):
    out_ref = rest[-1]
    head, far = ids[0], ids[1]
    pieces = (a_ref, b_ref, c_ref, d_ref)
    heads = (2 * far + head, 2 * far + 1 - head, 2 * (1 - far) + head, 2 * (1 - far) + 1 - head)
    total = None
    for piece in pieces:
        value = piece[...].astype(F32)
        square = jnp.sum(value * value, axis=1, keepdims=True)
        total = square if total is None else total + square
    scale = lax.rsqrt(total / (4 * HD) + EPS)
    for piece, place in zip(pieces, heads):
        columns = pl.ds(pl.multiple_of(place * HD, HD), HD)
        out_ref[0, :, columns] = (piece[...].astype(F32) * scale * gain_ref[0:1, columns]).astype(BF)


def normalise(ids, group, groups, pieces, gain, former):
    tokens = pieces[0].shape[0]
    part = pl.BlockSpec((tokens, HD), lambda i, ids: (0, 0))
    more = [] if former is None else [former]
    return pl.pallas_call(
        norm_kernel,
        out_shape=jax.ShapeDtypeStruct((groups, tokens, 4 * HD), BF),
        grid_spec=pltpu.PrefetchScalarGridSpec(
            num_scalar_prefetch=1,
            grid=(1,),
            in_specs=[part] * 4
            + [pl.BlockSpec((1, 4 * HD), lambda i, ids: (0, 0))]
            + [pl.BlockSpec(memory_space=pl.ANY)] * len(more),
            out_specs=pl.BlockSpec((1, tokens, 4 * HD), lambda i, ids: (group, 0, 0)),
        ),
        input_output_aliases={} if former is None else {6: 0},
        compiler_params=params(),
        cost_estimate=cost(8 * tokens * HD * 4, 4 * tokens * HD * 4),
    )(ids, *pieces, gain, *more)


SWAP = [(0, 1), (1, 0)]
BOTH = [(0, 3), (1, 2), (2, 1), (3, 0)]


def body(inputs, projections, lrate, fast_init, gain):
    groups = inputs.shape[0]
    plane = lax.axis_index("z_hi").astype(jnp.int32)
    core = lax.axis_index("core").astype(jnp.int32)
    far = lax.axis_index("head").astype(jnp.int32)
    kept = jnp.stack([plane, far])
    given = jnp.stack([1 - plane, far])
    share = jnp.stack([plane, core])
    gain = gain.reshape(1, -1)
    rates = lrate.transpose(0, 2, 1)

    def across(x):
        return lax.ppermute(x, "core", SWAP)

    def beyond(x):
        return lax.ppermute(x, "z_hi", SWAP)

    def after(ids, dep):
        return ids if dep is None else lax.optimization_barrier((ids, dep))[0]

    def of(ids, jobs, dep=None):
        return project(after(ids, dep), jobs, inputs, projections, rates)

    def forward(far_parts):
        return (
            lax.ppermute(far_parts[0], "head", SWAP),
            lax.ppermute(far_parts[1], ("z_hi", "head"), BOTH),
        )

    def to_rows(far_parts, near_parts):
        return near_parts[0], beyond(near_parts[1]), *forward(far_parts)

    def summed(grads, beside_sum=None, beside_gather=None):
        parts, first = exchange(grads, beside_sum)
        shard, squares = sum_shards(parts)
        shards, second = exchange(with_notes(shard, squares, across(squares)), beside_gather)
        return shards, first, second

    def readouts(memory, *asked):
        mate = across(memory)
        return read(1, memory, mate, *asked), read(0, memory, mate, *asked)

    later = ((1, 1), (1, 2), (1, 0), (0, 0))
    (given_now,) = of(given, ((0, 1), (0, 2)))
    foreign = beyond(given_now)
    (own,) = of(kept, ((0, 1), (0, 2)))
    own_mate = across(own)
    given_next, given_asked = of(given, later, own)
    memory, target = start_memory(after(share, given_next), fast_init)
    foreign, memory, given_next, given_asked = lax.optimization_barrier((foreign, memory, given_next, given_asked))
    foreign_next = beyond(given_next)
    foreign_asked = beyond(given_asked)
    pieces = (own, own_mate, foreign, across(foreign))
    grads = first_step(memory, pieces)
    shards, (own_next, own_asked), _ = summed(grads, lambda dep: tuple(of(kept, later, dep)))
    grads, memory = next_step(memory, shards, target, pieces)
    shards, (foreign_next, own_next_mate), (foreign_next_mate, foreign_asked) = summed(
        grads,
        lambda dep: (foreign_next, across(own_next)),
        lambda dep: (across(foreign_next), foreign_asked),
    )
    pieces = (own_next, own_next_mate, foreign_next, foreign_next_mate)

    grads, memory = next_step(memory, shards, target, pieces)
    then, mate = memory, across(memory)
    parts, first = exchange(grads, lambda dep: mate)
    shard, squares = sum_shards(parts)
    asked = (own_asked, 1, foreign_asked, 1)
    shards, (far_parts, near_parts) = exchange(
        with_notes(shard, squares, across(squares)),
        lambda dep: (read(1, then, first, *asked), read(0, then, first, *asked)),
    )
    ahead, askew = forward(far_parts)
    beside = beyond(near_parts[1])
    grads, memory = next_step(memory, shards, target, pieces)
    shards, beside, (ahead, askew) = summed(grads, lambda dep: beside, lambda dep: (ahead, askew))
    rows_then = (near_parts[0], beside, ahead, askew)
    memory = last_memory(memory, shards, target)
    rows = to_rows(*readouts(memory, own_asked, 0, foreign_asked, 0))
    result = normalise(after(kept, memory), 0, groups, rows_then, gain, None)
    return normalise(kept, 1, groups, rows, gain, result)


def solution(mesh):
    finer = Mesh(
        mesh.devices.reshape(4, 2, 4, 2, mesh.shape["head"]),
        (*TOK, "head"),
    )
    placed = (
        P(None, TOK, None),
        P(None, None, "head"),
        P(None, TOK, "head"),
        P("head", None, None, None),
        P(),
    )
    return jax.shard_map(
        body, mesh=finer, in_specs=placed, out_specs=P(None, (*TOK, "head"), None), check_vma=False
    )
```

```python
import functools

import jax
import jax.numpy as jnp
from jax import lax
from jax.experimental import pallas as pl
from jax.experimental.pallas import tpu as pltpu
from jax.sharding import Mesh
from jax.sharding import PartitionSpec as P

STEP_SIZE = 4.0
EPS = 1e-06
TOK = ("y", "z_hi", "x", "core")
PLANE = ("y", "x")
PEERS = 16
HD = 512
F = 192
ROWS = 48
COLS = 128
SHARD = 3 * ROWS
NOTE = 16
CHUNK = 256
DEPTHS = 4
AHEAD = 8
BF = jnp.bfloat16
F32 = jnp.float32
MIB = 1024 * 1024


def params(limit=24):
    return pltpu.CompilerParams(vmem_limit_bytes=limit * MIB)


def cost(flops, moved):
    return pl.CostEstimate(flops=int(flops), bytes_accessed=int(moved), transcendentals=0)


def nt(left, right):
    return lax.dot_general(left, right, (((1,), (1,)), ((), ())), preferred_element_type=F32)


def nn(left, right):
    return lax.dot_general(left, right, (((1,), (0,)), ((), ())), preferred_element_type=F32)


def project_kernel(jobs, ids, x_ref, w_ref, rate_ref, *rest):
    *outs, x_buf, w_buf, x_sem, w_sem = rest
    groups = sorted({group for group, _ in jobs})
    kinds = sorted({kind for _, kind in jobs})
    depth = x_buf.shape[2] // DEPTHS
    half = x_buf.shape[1] // 2
    columns = pl.ds(pl.multiple_of(ids[0] * HD, HD), HD)
    copies = []
    for k in range(DEPTHS):
        part = pl.ds(k * depth, depth)
        some = []
        for g, group in enumerate(groups):
            for h, place in enumerate((ids[1], 1 - ids[1])):
                source = x_ref.at[group, pl.ds(pl.multiple_of(place * half, half), half), part]
                target = x_buf.at[g, pl.ds(h * half, half), part]
                some.append(pltpu.make_async_copy(source, target, x_sem.at[g, h, k]))
        for m, kind in enumerate(kinds):
            source = w_ref.at[kind, part, columns]
            some.append(pltpu.make_async_copy(source, w_buf.at[m, part, :], w_sem.at[m, k]))
        for copy in some:
            copy.start()
        copies.append(some)
    totals = [None] * len(jobs)
    for k in range(DEPTHS):
        for copy in copies[k]:
            copy.wait()
        part = slice(k * depth, (k + 1) * depth)
        for n, (group, kind) in enumerate(jobs):
            term = nn(x_buf[groups.index(group), :, part], w_buf[kinds.index(kind), part, :])
            totals[n] = term if k == 0 else totals[n] + term
    for n, (group, kind) in enumerate(jobs):
        result = totals[n].astype(BF)
        if kind == 2:
            rates = jnp.where(ids[0] == 0, rate_ref[group, 0:1, :], rate_ref[group, 1:2, :])
            low, high = rates[:, 0:half], rates[:, half : 2 * half]
            rates = jnp.concatenate(
                [jnp.where(ids[1] == 0, low, high), jnp.where(ids[1] == 0, high, low)], axis=1
            )
            rates = jnp.transpose(jnp.broadcast_to(rates, (8, 2 * half)))[:, 0:1]
            result = (-rates * result.astype(F32)).astype(BF)
        outs[n // 2][:, n % 2 * HD : (n % 2 + 1) * HD] = result


def project(ids, jobs, inputs, projections, rates):
    tokens, width = inputs.shape[1:]
    groups = len({group for group, _ in jobs})
    kinds = len({kind for _, kind in jobs})
    count = len(jobs)
    return pl.pallas_call(
        functools.partial(project_kernel, jobs),
        out_shape=[jax.ShapeDtypeStruct((tokens, 2 * HD), BF)] * (count // 2),
        grid_spec=pltpu.PrefetchScalarGridSpec(
            num_scalar_prefetch=1,
            grid=(1,),
            in_specs=[
                pl.BlockSpec(memory_space=pltpu.HBM),
                pl.BlockSpec(memory_space=pltpu.HBM),
                pl.BlockSpec(rates.shape, lambda i, ids: (0, 0, 0)),
            ],
            out_specs=[pl.BlockSpec((tokens, 2 * HD), lambda i, ids: (0, 0))] * (count // 2),
            scratch_shapes=[
                pltpu.VMEM((groups, tokens, width), BF),
                pltpu.VMEM((kinds, width, HD), BF),
                pltpu.SemaphoreType.DMA((groups, 2, DEPTHS)),
                pltpu.SemaphoreType.DMA((kinds, DEPTHS)),
            ],
        ),
        compiler_params=params(46),
        cost_estimate=cost(2 * count * tokens * width * HD, 2 * groups * tokens * width + 2 * kinds * width * HD),
    )(ids, inputs, projections, rates)


def fetches(pieces, ks_buf, sem):
    copies = []
    for piece in pieces:
        for first in range(0, piece.shape[0], CHUNK):
            n = len(copies)
            source = piece.at[pl.ds(first, CHUNK), pl.ds(0, 2 * HD)]
            copies.append(pltpu.make_async_copy(source, ks_buf.at[pl.ds(n * CHUNK, CHUNK), :], sem.at[n]))
    for copy in copies[:AHEAD]:
        copy.start()
    return copies


def gradients(w_ref, copies, ks_buf, d_ref, out_ref):
    for n, copy in enumerate(copies):
        copy.wait()
        if n + AHEAD < len(copies):
            copies[n + AHEAD].start()
        some = slice(n * CHUNK, (n + 1) * CHUNK)
        both = nt(w_ref[0 : 2 * F, :], ks_buf[some, 0:HD])
        back = nt(w_ref[2 * F : 3 * F, :], ks_buf[some, HD : 2 * HD])
        hidden, gated = both[0:F, :], both[F : 2 * F, :]
        sigma = 0.5 * jnp.tanh(0.5 * hidden) + 0.5
        act = hidden * sigma
        d_ref[0:F, some] = (back * gated * (sigma + act * (1.0 - sigma))).astype(BF)
        d_ref[F : 2 * F, some] = (back * act).astype(BF)
        d_ref[2 * F : 3 * F, some] = (act * gated).astype(BF)
    grads = [nn(d_ref[0 : 2 * F, :], ks_buf[:, 0:HD]).astype(BF)]
    grads.append(nn(d_ref[2 * F : 3 * F, :], ks_buf[:, HD : 2 * HD]).astype(BF))
    for m in range(3):
        for r in range(F // ROWS):
            first = (m % 2) * F * (m < 2) + r * ROWS
            for c in range(HD // COLS):
                out_ref[r * (HD // COLS) + c, m * ROWS : (m + 1) * ROWS, :] = grads[m // 2][
                    first : first + ROWS, c * COLS : (c + 1) * COLS
                ]


def renew(w_ref, shards_ref, target_ref, new_ref):
    notes = shards_ref[0, SHARD : SHARD + NOTE, :].astype(F32)
    for i in range(1, PEERS):
        notes += shards_ref[i, SHARD : SHARD + NOTE, :].astype(F32)
    for m in range(3):
        frob = notes[3 * m : 3 * m + 1, :] + notes[3 * m + 1 : 3 * m + 2, :] + notes[3 * m + 2 : 3 * m + 3, :]
        scale = STEP_SIZE * lax.rsqrt(frob + EPS)
        for r in range(F // ROWS):
            rows = slice(m * F + r * ROWS, m * F + (r + 1) * ROWS)
            updates = []
            total = None
            for c in range(HD // COLS):
                grad = shards_ref[r * (HD // COLS) + c, m * ROWS : (m + 1) * ROWS, :].astype(F32)
                update = w_ref[rows, c * COLS : (c + 1) * COLS].astype(F32) - scale * grad
                updates.append(update)
                total = update * update if total is None else total + update * update
            length = jnp.sum(total, axis=1, keepdims=True)
            factor = target_ref[rows, :] * lax.rsqrt(length + EPS)
            for c in range(HD // COLS):
                new_ref[rows, c * COLS : (c + 1) * COLS] = (updates[c] * factor).astype(BF)


def start_kernel(ids, init_ref, w_ref, target_ref):
    for m in range(3):
        rows = slice(m * F, (m + 1) * F)
        start = init_ref[0, m]
        w_ref[rows, :] = start
        start = start.astype(F32)
        length = jnp.sqrt(jnp.sum(start * start, axis=1, keepdims=True))
        target_ref[rows, :] = jnp.broadcast_to(length, (F, COLS))


def first_step_kernel(w_ref, *rest):
    *pieces, out_ref, ks_buf, d_ref, sem = rest
    copies = fetches(pieces, ks_buf, sem)
    gradients(w_ref, copies, ks_buf, d_ref, out_ref)


def next_step_kernel(old_ref, shards_ref, target_ref, *rest):
    *pieces, out_ref, w_ref, ks_buf, d_ref, sem = rest
    copies = fetches(pieces, ks_buf, sem)
    renew(old_ref, shards_ref, target_ref, w_ref)
    gradients(w_ref, copies, ks_buf, d_ref, out_ref)


def renew_kernel(old_ref, shards_ref, target_ref, w_ref):
    renew(old_ref, shards_ref, target_ref, w_ref)


GRADS = jax.ShapeDtypeStruct((PEERS, SHARD, COLS), BF)
MEMORY = jax.ShapeDtypeStruct((3 * F, HD), BF)
TARGET = jax.ShapeDtypeStruct((3 * F, COLS), F32)
SQUARES = jax.ShapeDtypeStruct((8, COLS), F32)


def step_scratch(pieces):
    tokens = sum(piece.shape[0] for piece in pieces)
    return [
        pltpu.VMEM((tokens, 2 * HD), BF),
        pltpu.VMEM((3 * F, tokens), BF),
        pltpu.SemaphoreType.DMA((tokens // CHUNK,)),
    ]


def step_cost(pieces):
    tokens = sum(piece.shape[0] for piece in pieces)
    return cost(12 * tokens * F * HD, 8 << 20)


def start_memory(ids, fast_init):
    return pl.pallas_call(
        start_kernel,
        out_shape=(MEMORY, TARGET),
        grid_spec=pltpu.PrefetchScalarGridSpec(
            num_scalar_prefetch=1,
            grid=(1,),
            in_specs=[pl.BlockSpec((1, 3, F, HD), lambda i, ids: (ids[0], 0, ids[1], 0))],
            out_specs=(
                pl.BlockSpec(MEMORY.shape, lambda i, ids: (0, 0)),
                pl.BlockSpec(TARGET.shape, lambda i, ids: (0, 0)),
            ),
        ),
        compiler_params=params(),
        cost_estimate=cost(9 * F * HD, 4 << 20),
    )(ids, fast_init)


def first_step(memory, pieces):
    whole = pl.BlockSpec(memory_space=pltpu.VMEM)
    return pl.pallas_call(
        first_step_kernel,
        out_shape=GRADS,
        in_specs=[whole] + [pl.BlockSpec(memory_space=pltpu.HBM)] * len(pieces),
        out_specs=whole,
        scratch_shapes=step_scratch(pieces),
        compiler_params=params(),
        cost_estimate=step_cost(pieces),
    )(memory, *pieces)


def next_step(old, shards, target, pieces):
    whole = pl.BlockSpec(memory_space=pltpu.VMEM)
    return pl.pallas_call(
        next_step_kernel,
        out_shape=(GRADS, MEMORY),
        in_specs=[whole] * 3 + [pl.BlockSpec(memory_space=pltpu.HBM)] * len(pieces),
        out_specs=(whole, whole),
        scratch_shapes=step_scratch(pieces),
        compiler_params=params(),
        cost_estimate=step_cost(pieces),
    )(old, shards, target, *pieces)


def last_memory(old, shards, target):
    return pl.pallas_call(
        renew_kernel,
        out_shape=MEMORY,
        compiler_params=params(),
        cost_estimate=cost(8 * old.size, 6 * old.size),
    )(old, shards, target)


def sum_kernel(parts_ref, out_ref, squares_ref):
    total = parts_ref[0].astype(F32)
    for i in range(1, PEERS):
        total += parts_ref[i].astype(F32)
    out_ref[...] = total.astype(BF)
    row = lax.broadcasted_iota(jnp.int32, SQUARES.shape, 0)
    squares = jnp.zeros(SQUARES.shape, F32)
    for m in range(3):
        part = total[m * ROWS : (m + 1) * ROWS, :]
        squares = jnp.where(row == m, jnp.sum(part * part, keepdims=True), squares)
    squares_ref[...] = squares


def sum_shards(parts):
    return pl.pallas_call(
        sum_kernel,
        out_shape=(jax.ShapeDtypeStruct((SHARD, COLS), BF), SQUARES),
        compiler_params=params(),
        cost_estimate=cost(2 * parts.size, 2 * parts.size),
    )(parts)


def note_kernel(shard_ref, here_ref, there_ref, out_ref):
    squares = here_ref[...] + there_ref[...]
    row = lax.broadcasted_iota(jnp.int32, (NOTE, COLS), 0)
    notes = jnp.zeros((NOTE, COLS), F32)
    for m in range(3):
        left = jnp.broadcast_to(squares[m : m + 1, :], (NOTE, COLS))
        for piece in range(3):
            term = left.astype(BF).astype(F32)
            notes = jnp.where(row == 3 * m + piece, term, notes)
            left = left - term
    notes = notes.astype(BF)
    shard = shard_ref[...]
    for i in range(PEERS):
        out_ref[i, 0:SHARD, :] = shard
        out_ref[i, SHARD : SHARD + NOTE, :] = notes


def with_notes(shard, here, there):
    return pl.pallas_call(
        note_kernel,
        out_shape=jax.ShapeDtypeStruct((PEERS, SHARD + NOTE, COLS), BF),
        compiler_params=params(),
        cost_estimate=cost(4 * shard.size, 2 * PEERS * shard.size),
    )(shard, here, there)


def exchange(x, beside):
    moved = lax.all_to_all(x, PLANE, 0, 0, tiled=True)
    if beside is None:
        return moved, None
    return lax.optimization_barrier((moved, beside(x)))


def read_kernel(here_ref, there_ref, *rest):
    count = len(rest) // 2
    for queries_ref, out_ref in zip(rest[:count], rest[count:]):
        queries = queries_ref[...]
        total = None
        for w_ref in (here_ref, there_ref):
            hidden = nt(queries, w_ref[0:F, :])
            gated = nt(queries, w_ref[F : 2 * F, :])
            sigma = 0.5 * jnp.tanh(0.5 * hidden) + 0.5
            mixed = (hidden * sigma * gated).astype(BF)
            term = nn(mixed, w_ref[2 * F : 3 * F, :])
            total = term if total is None else total + term
        out_ref[...] = total.astype(BF)


def read(half, here, there, own, own_place, foreign, foreign_place):
    tokens = own.shape[0] // 2
    memory = pl.BlockSpec(MEMORY.shape, lambda i: (0, 0))
    back = pl.BlockSpec((tokens, HD), lambda i: (0, 0))
    out = jax.ShapeDtypeStruct((tokens, HD), BF)
    return pl.pallas_call(
        read_kernel,
        out_shape=(out, out),
        grid=(1,),
        in_specs=[
            memory,
            memory,
            pl.BlockSpec((tokens, HD), lambda i: (half, own_place)),
            pl.BlockSpec((tokens, HD), lambda i: (half, foreign_place)),
        ],
        out_specs=(back, back),
        compiler_params=params(),
        cost_estimate=cost(24 * tokens * F * HD, 4 << 20),
    )(here, there, own, foreign)


def norm_kernel(ids, a_ref, b_ref, c_ref, d_ref, gain_ref, *rest):
    out_ref = rest[-1]
    head, far = ids[0], ids[1]
    pieces = (a_ref, b_ref, c_ref, d_ref)
    heads = (2 * far + head, 2 * far + 1 - head, 2 * (1 - far) + head, 2 * (1 - far) + 1 - head)
    total = None
    for piece in pieces:
        value = piece[...].astype(F32)
        square = jnp.sum(value * value, axis=1, keepdims=True)
        total = square if total is None else total + square
    scale = lax.rsqrt(total / (4 * HD) + EPS)
    for piece, place in zip(pieces, heads):
        columns = pl.ds(pl.multiple_of(place * HD, HD), HD)
        out_ref[0, :, columns] = (piece[...].astype(F32) * scale * gain_ref[0:1, columns]).astype(BF)


def normalise(ids, group, groups, pieces, gain, former):
    tokens = pieces[0].shape[0]
    part = pl.BlockSpec((tokens, HD), lambda i, ids: (0, 0))
    more = [] if former is None else [former]
    return pl.pallas_call(
        norm_kernel,
        out_shape=jax.ShapeDtypeStruct((groups, tokens, 4 * HD), BF),
        grid_spec=pltpu.PrefetchScalarGridSpec(
            num_scalar_prefetch=1,
            grid=(1,),
            in_specs=[part] * 4
            + [pl.BlockSpec((1, 4 * HD), lambda i, ids: (0, 0))]
            + [pl.BlockSpec(memory_space=pl.ANY)] * len(more),
            out_specs=pl.BlockSpec((1, tokens, 4 * HD), lambda i, ids: (group, 0, 0)),
        ),
        input_output_aliases={} if former is None else {6: 0},
        compiler_params=params(),
        cost_estimate=cost(8 * tokens * HD * 4, 4 * tokens * HD * 4),
    )(ids, *pieces, gain, *more)


SWAP = [(0, 1), (1, 0)]
BOTH = [(0, 3), (1, 2), (2, 1), (3, 0)]


def body(inputs, projections, lrate, fast_init, gain):
    groups = inputs.shape[0]
    plane = lax.axis_index("z_hi").astype(jnp.int32)
    core = lax.axis_index("core").astype(jnp.int32)
    far = lax.axis_index("head").astype(jnp.int32)
    kept = jnp.stack([plane, far])
    given = jnp.stack([1 - plane, far])
    share = jnp.stack([plane, core])
    gain = gain.reshape(1, -1)
    rates = lrate.transpose(0, 2, 1)

    def across(x):
        return lax.ppermute(x, "core", SWAP)

    def beyond(x):
        return lax.ppermute(x, "z_hi", SWAP)

    def after(ids, dep):
        return ids if dep is None else lax.optimization_barrier((ids, dep))[0]

    def of(ids, jobs, dep=None):
        return project(after(ids, dep), jobs, inputs, projections, rates)

    def forward(far_parts):
        return (
            lax.ppermute(far_parts[0], "head", SWAP),
            lax.ppermute(far_parts[1], ("z_hi", "head"), BOTH),
        )

    def to_rows(far_parts, near_parts):
        return near_parts[0], beyond(near_parts[1]), *forward(far_parts)

    def summed(grads, beside_sum=None, beside_gather=None):
        parts, first = exchange(grads, beside_sum)
        shard, squares = sum_shards(parts)
        shards, second = exchange(with_notes(shard, squares, across(squares)), beside_gather)
        return shards, first, second

    def readouts(memory, *asked):
        mate = across(memory)
        return read(1, memory, mate, *asked), read(0, memory, mate, *asked)

    later = ((1, 1), (1, 2), (1, 0), (0, 0))
    (given_now,) = of(given, ((0, 1), (0, 2)))
    foreign = beyond(given_now)
    (own,) = of(kept, ((0, 1), (0, 2)))
    own_mate = across(own)
    given_next, given_asked = of(given, later, own)
    memory, target = start_memory(after(share, given_next), fast_init)
    foreign, memory, given_next, given_asked = lax.optimization_barrier((foreign, memory, given_next, given_asked))
    foreign_next = beyond(given_next)
    foreign_asked = beyond(given_asked)
    pieces = (own, own_mate, foreign, across(foreign))
    grads = first_step(memory, pieces)
    shards, (own_next, own_asked), _ = summed(grads, lambda dep: tuple(of(kept, later, dep)))
    grads, memory = next_step(memory, shards, target, pieces)
    shards, (foreign_next, own_next_mate), (foreign_next_mate, foreign_asked) = summed(
        grads,
        lambda dep: (foreign_next, across(own_next)),
        lambda dep: (across(foreign_next), foreign_asked),
    )
    pieces = (own_next, own_next_mate, foreign_next, foreign_next_mate)

    grads, memory = next_step(memory, shards, target, pieces)
    then, mate = memory, across(memory)
    parts, first = exchange(grads, lambda dep: mate)
    shard, squares = sum_shards(parts)
    asked = (own_asked, 1, foreign_asked, 1)
    far_parts, near_parts = read(1, then, first, *asked), read(0, then, first, *asked)
    message = with_notes(shard, squares, across(squares))
    message, far_parts, near_parts = lax.optimization_barrier((message, far_parts, near_parts))
    shards, _ = exchange(message, None)
    ahead, askew = forward(far_parts)
    beside = beyond(near_parts[1])
    grads, memory = next_step(memory, shards, target, pieces)
    shards, beside, (ahead, askew) = summed(grads, lambda dep: beside, lambda dep: (ahead, askew))
    rows_then = (near_parts[0], beside, ahead, askew)
    memory = last_memory(memory, shards, target)
    rows = to_rows(*readouts(memory, own_asked, 0, foreign_asked, 0))
    result = normalise(after(kept, memory), 0, groups, rows_then, gain, None)
    return normalise(kept, 1, groups, rows, gain, result)


def solution(mesh):
    finer = Mesh(
        mesh.devices.reshape(4, 2, 4, 2, mesh.shape["head"]),
        (*TOK, "head"),
    )
    placed = (
        P(None, TOK, None),
        P(None, None, "head"),
        P(None, TOK, "head"),
        P("head", None, None, None),
        P(),
    )
    return jax.shard_map(
        body, mesh=finer, in_specs=placed, out_specs=P(None, (*TOK, "head"), None), check_vma=False
    )
```

```python
import functools

import jax
import jax.numpy as jnp
from jax import lax
from jax.experimental import pallas as pl
from jax.experimental.pallas import tpu as pltpu
from jax.sharding import Mesh
from jax.sharding import PartitionSpec as P

STEP_SIZE = 4.0
EPS = 1e-06
TOK = ("y", "z_hi", "x", "core")
PLANE = ("y", "x")
PEERS = 16
HD = 512
F = 192
ROWS = 48
COLS = 128
SHARD = 3 * ROWS
NOTE = 16
CHUNK = 256
DEPTHS = 4
AHEAD = 8
BF = jnp.bfloat16
F32 = jnp.float32
MIB = 1024 * 1024


def params(limit=24):
    return pltpu.CompilerParams(vmem_limit_bytes=limit * MIB)


def cost(flops, moved):
    return pl.CostEstimate(flops=int(flops), bytes_accessed=int(moved), transcendentals=0)


def nt(left, right):
    return lax.dot_general(left, right, (((1,), (1,)), ((), ())), preferred_element_type=F32)


def nn(left, right):
    return lax.dot_general(left, right, (((1,), (0,)), ((), ())), preferred_element_type=F32)


def project_kernel(jobs, ids, x_ref, w_ref, rate_ref, *rest):
    *outs, x_buf, w_buf, x_sem, w_sem = rest
    groups = sorted({group for group, _ in jobs})
    kinds = sorted({kind for _, kind in jobs})
    depth = x_buf.shape[2] // DEPTHS
    half = x_buf.shape[1] // 2
    columns = pl.ds(pl.multiple_of(ids[0] * HD, HD), HD)
    copies = []
    for k in range(DEPTHS):
        part = pl.ds(k * depth, depth)
        some = []
        for g, group in enumerate(groups):
            for h, place in enumerate((ids[1], 1 - ids[1])):
                source = x_ref.at[group, pl.ds(pl.multiple_of(place * half, half), half), part]
                target = x_buf.at[g, pl.ds(h * half, half), part]
                some.append(pltpu.make_async_copy(source, target, x_sem.at[g, h, k]))
        for m, kind in enumerate(kinds):
            source = w_ref.at[kind, part, columns]
            some.append(pltpu.make_async_copy(source, w_buf.at[m, part, :], w_sem.at[m, k]))
        for copy in some:
            copy.start()
        copies.append(some)
    totals = [None] * len(jobs)
    for k in range(DEPTHS):
        for copy in copies[k]:
            copy.wait()
        part = slice(k * depth, (k + 1) * depth)
        for n, (group, kind) in enumerate(jobs):
            term = nn(x_buf[groups.index(group), :, part], w_buf[kinds.index(kind), part, :])
            totals[n] = term if k == 0 else totals[n] + term
    for n, (group, kind) in enumerate(jobs):
        result = totals[n].astype(BF)
        if kind == 2:
            rates = jnp.where(ids[0] == 0, rate_ref[group, 0:1, :], rate_ref[group, 1:2, :])
            low, high = rates[:, 0:half], rates[:, half : 2 * half]
            rates = jnp.concatenate(
                [jnp.where(ids[1] == 0, low, high), jnp.where(ids[1] == 0, high, low)], axis=1
            )
            rates = jnp.transpose(jnp.broadcast_to(rates, (8, 2 * half)))[:, 0:1]
            result = (-rates * result.astype(F32)).astype(BF)
        outs[n // 2][:, n % 2 * HD : (n % 2 + 1) * HD] = result


def project(ids, jobs, inputs, projections, rates):
    tokens, width = inputs.shape[1:]
    groups = len({group for group, _ in jobs})
    kinds = len({kind for _, kind in jobs})
    count = len(jobs)
    return pl.pallas_call(
        functools.partial(project_kernel, jobs),
        out_shape=[jax.ShapeDtypeStruct((tokens, 2 * HD), BF)] * (count // 2),
        grid_spec=pltpu.PrefetchScalarGridSpec(
            num_scalar_prefetch=1,
            grid=(1,),
            in_specs=[
                pl.BlockSpec(memory_space=pltpu.HBM),
                pl.BlockSpec(memory_space=pltpu.HBM),
                pl.BlockSpec(rates.shape, lambda i, ids: (0, 0, 0)),
            ],
            out_specs=[pl.BlockSpec((tokens, 2 * HD), lambda i, ids: (0, 0))] * (count // 2),
            scratch_shapes=[
                pltpu.VMEM((groups, tokens, width), BF),
                pltpu.VMEM((kinds, width, HD), BF),
                pltpu.SemaphoreType.DMA((groups, 2, DEPTHS)),
                pltpu.SemaphoreType.DMA((kinds, DEPTHS)),
            ],
        ),
        compiler_params=params(46),
        cost_estimate=cost(2 * count * tokens * width * HD, 2 * groups * tokens * width + 2 * kinds * width * HD),
    )(ids, inputs, projections, rates)


def fetches(pieces, ks_buf, sem):
    copies = []
    for piece in pieces:
        for first in range(0, piece.shape[0], CHUNK):
            n = len(copies)
            source = piece.at[pl.ds(first, CHUNK), pl.ds(0, 2 * HD)]
            copies.append(pltpu.make_async_copy(source, ks_buf.at[pl.ds(n * CHUNK, CHUNK), :], sem.at[n]))
    for copy in copies[:AHEAD]:
        copy.start()
    return copies


def gradients(w_ref, copies, ks_buf, d_ref, out_ref):
    for n, copy in enumerate(copies):
        copy.wait()
        if n + AHEAD < len(copies):
            copies[n + AHEAD].start()
        some = slice(n * CHUNK, (n + 1) * CHUNK)
        both = nt(w_ref[0 : 2 * F, :], ks_buf[some, 0:HD])
        back = nt(w_ref[2 * F : 3 * F, :], ks_buf[some, HD : 2 * HD])
        hidden, gated = both[0:F, :], both[F : 2 * F, :]
        sigma = 0.5 * jnp.tanh(0.5 * hidden) + 0.5
        act = hidden * sigma
        d_ref[0:F, some] = (back * gated * (sigma + act * (1.0 - sigma))).astype(BF)
        d_ref[F : 2 * F, some] = (back * act).astype(BF)
        d_ref[2 * F : 3 * F, some] = (act * gated).astype(BF)
    grads = [nn(d_ref[0 : 2 * F, :], ks_buf[:, 0:HD]).astype(BF)]
    grads.append(nn(d_ref[2 * F : 3 * F, :], ks_buf[:, HD : 2 * HD]).astype(BF))
    for m in range(3):
        for r in range(F // ROWS):
            first = (m % 2) * F * (m < 2) + r * ROWS
            for c in range(HD // COLS):
                out_ref[r * (HD // COLS) + c, m * ROWS : (m + 1) * ROWS, :] = grads[m // 2][
                    first : first + ROWS, c * COLS : (c + 1) * COLS
                ]


def renew(w_ref, shards_ref, target_ref, new_ref):
    notes = shards_ref[0, SHARD : SHARD + NOTE, :].astype(F32)
    for i in range(1, PEERS):
        notes += shards_ref[i, SHARD : SHARD + NOTE, :].astype(F32)
    for m in range(3):
        frob = notes[3 * m : 3 * m + 1, :] + notes[3 * m + 1 : 3 * m + 2, :] + notes[3 * m + 2 : 3 * m + 3, :]
        scale = STEP_SIZE * lax.rsqrt(frob + EPS)
        for r in range(F // ROWS):
            rows = slice(m * F + r * ROWS, m * F + (r + 1) * ROWS)
            updates = []
            total = None
            for c in range(HD // COLS):
                grad = shards_ref[r * (HD // COLS) + c, m * ROWS : (m + 1) * ROWS, :].astype(F32)
                update = w_ref[rows, c * COLS : (c + 1) * COLS].astype(F32) - scale * grad
                updates.append(update)
                total = update * update if total is None else total + update * update
            length = jnp.sum(total, axis=1, keepdims=True)
            factor = target_ref[rows, :] * lax.rsqrt(length + EPS)
            for c in range(HD // COLS):
                new_ref[rows, c * COLS : (c + 1) * COLS] = (updates[c] * factor).astype(BF)


def start_kernel(ids, init_ref, w_ref, target_ref):
    for m in range(3):
        rows = slice(m * F, (m + 1) * F)
        start = init_ref[0, m]
        w_ref[rows, :] = start
        start = start.astype(F32)
        length = jnp.sqrt(jnp.sum(start * start, axis=1, keepdims=True))
        target_ref[rows, :] = jnp.broadcast_to(length, (F, COLS))


def first_step_kernel(w_ref, *rest):
    *pieces, out_ref, ks_buf, d_ref, sem = rest
    copies = fetches(pieces, ks_buf, sem)
    gradients(w_ref, copies, ks_buf, d_ref, out_ref)


def next_step_kernel(old_ref, shards_ref, target_ref, *rest):
    *pieces, out_ref, w_ref, ks_buf, d_ref, sem = rest
    copies = fetches(pieces, ks_buf, sem)
    renew(old_ref, shards_ref, target_ref, w_ref)
    gradients(w_ref, copies, ks_buf, d_ref, out_ref)


def renew_kernel(old_ref, shards_ref, target_ref, w_ref):
    renew(old_ref, shards_ref, target_ref, w_ref)


GRADS = jax.ShapeDtypeStruct((PEERS, SHARD, COLS), BF)
MEMORY = jax.ShapeDtypeStruct((3 * F, HD), BF)
TARGET = jax.ShapeDtypeStruct((3 * F, COLS), F32)
SQUARES = jax.ShapeDtypeStruct((8, COLS), F32)


def step_scratch(pieces):
    tokens = sum(piece.shape[0] for piece in pieces)
    return [
        pltpu.VMEM((tokens, 2 * HD), BF),
        pltpu.VMEM((3 * F, tokens), BF),
        pltpu.SemaphoreType.DMA((tokens // CHUNK,)),
    ]


def step_cost(pieces):
    tokens = sum(piece.shape[0] for piece in pieces)
    return cost(12 * tokens * F * HD, 8 << 20)


def start_memory(ids, fast_init):
    return pl.pallas_call(
        start_kernel,
        out_shape=(MEMORY, TARGET),
        grid_spec=pltpu.PrefetchScalarGridSpec(
            num_scalar_prefetch=1,
            grid=(1,),
            in_specs=[pl.BlockSpec((1, 3, F, HD), lambda i, ids: (ids[0], 0, ids[1], 0))],
            out_specs=(
                pl.BlockSpec(MEMORY.shape, lambda i, ids: (0, 0)),
                pl.BlockSpec(TARGET.shape, lambda i, ids: (0, 0)),
            ),
        ),
        compiler_params=params(),
        cost_estimate=cost(9 * F * HD, 4 << 20),
    )(ids, fast_init)


def first_step(memory, pieces):
    whole = pl.BlockSpec(memory_space=pltpu.VMEM)
    return pl.pallas_call(
        first_step_kernel,
        out_shape=GRADS,
        in_specs=[whole] + [pl.BlockSpec(memory_space=pltpu.HBM)] * len(pieces),
        out_specs=whole,
        scratch_shapes=step_scratch(pieces),
        compiler_params=params(),
        cost_estimate=step_cost(pieces),
    )(memory, *pieces)


def next_step(old, shards, target, pieces):
    whole = pl.BlockSpec(memory_space=pltpu.VMEM)
    return pl.pallas_call(
        next_step_kernel,
        out_shape=(GRADS, MEMORY),
        in_specs=[whole] * 3 + [pl.BlockSpec(memory_space=pltpu.HBM)] * len(pieces),
        out_specs=(whole, whole),
        scratch_shapes=step_scratch(pieces),
        compiler_params=params(),
        cost_estimate=step_cost(pieces),
    )(old, shards, target, *pieces)


def last_memory(old, shards, target):
    return pl.pallas_call(
        renew_kernel,
        out_shape=MEMORY,
        compiler_params=params(),
        cost_estimate=cost(8 * old.size, 6 * old.size),
    )(old, shards, target)


def sum_kernel(parts_ref, out_ref, squares_ref):
    total = parts_ref[0].astype(F32)
    for i in range(1, PEERS):
        total += parts_ref[i].astype(F32)
    out_ref[...] = total.astype(BF)
    row = lax.broadcasted_iota(jnp.int32, SQUARES.shape, 0)
    squares = jnp.zeros(SQUARES.shape, F32)
    for m in range(3):
        part = total[m * ROWS : (m + 1) * ROWS, :]
        squares = jnp.where(row == m, jnp.sum(part * part, keepdims=True), squares)
    squares_ref[...] = squares


def sum_shards(parts):
    return pl.pallas_call(
        sum_kernel,
        out_shape=(jax.ShapeDtypeStruct((SHARD, COLS), BF), SQUARES),
        compiler_params=params(),
        cost_estimate=cost(2 * parts.size, 2 * parts.size),
    )(parts)


def note_kernel(shard_ref, here_ref, there_ref, out_ref):
    squares = here_ref[...] + there_ref[...]
    row = lax.broadcasted_iota(jnp.int32, (NOTE, COLS), 0)
    notes = jnp.zeros((NOTE, COLS), F32)
    for m in range(3):
        left = jnp.broadcast_to(squares[m : m + 1, :], (NOTE, COLS))
        for piece in range(3):
            term = left.astype(BF).astype(F32)
            notes = jnp.where(row == 3 * m + piece, term, notes)
            left = left - term
    notes = notes.astype(BF)
    shard = shard_ref[...]
    for i in range(PEERS):
        out_ref[i, 0:SHARD, :] = shard
        out_ref[i, SHARD : SHARD + NOTE, :] = notes


def with_notes(shard, here, there):
    return pl.pallas_call(
        note_kernel,
        out_shape=jax.ShapeDtypeStruct((PEERS, SHARD + NOTE, COLS), BF),
        compiler_params=params(),
        cost_estimate=cost(4 * shard.size, 2 * PEERS * shard.size),
    )(shard, here, there)


def exchange(x, beside):
    moved = lax.all_to_all(x, PLANE, 0, 0, tiled=True)
    if beside is None:
        return moved, None
    return lax.optimization_barrier((moved, beside(x)))


def read_kernel(here_ref, there_ref, *rest):
    count = len(rest) // 2
    for queries_ref, out_ref in zip(rest[:count], rest[count:]):
        queries = queries_ref[...]
        total = None
        for w_ref in (here_ref, there_ref):
            hidden = nt(queries, w_ref[0:F, :])
            gated = nt(queries, w_ref[F : 2 * F, :])
            sigma = 0.5 * jnp.tanh(0.5 * hidden) + 0.5
            mixed = (hidden * sigma * gated).astype(BF)
            term = nn(mixed, w_ref[2 * F : 3 * F, :])
            total = term if total is None else total + term
        out_ref[...] = total.astype(BF)


def read(half, here, there, own, own_place, foreign, foreign_place):
    tokens = own.shape[0] // 2
    memory = pl.BlockSpec(MEMORY.shape, lambda i: (0, 0))
    back = pl.BlockSpec((tokens, HD), lambda i: (0, 0))
    out = jax.ShapeDtypeStruct((tokens, HD), BF)
    return pl.pallas_call(
        read_kernel,
        out_shape=(out, out),
        grid=(1,),
        in_specs=[
            memory,
            memory,
            pl.BlockSpec((tokens, HD), lambda i: (half, own_place)),
            pl.BlockSpec((tokens, HD), lambda i: (half, foreign_place)),
        ],
        out_specs=(back, back),
        compiler_params=params(),
        cost_estimate=cost(24 * tokens * F * HD, 4 << 20),
    )(here, there, own, foreign)


def norm_kernel(ids, a_ref, b_ref, c_ref, d_ref, gain_ref, *rest):
    out_ref = rest[-1]
    head, far = ids[0], ids[1]
    pieces = (a_ref, b_ref, c_ref, d_ref)
    heads = (2 * far + head, 2 * far + 1 - head, 2 * (1 - far) + head, 2 * (1 - far) + 1 - head)
    total = None
    for piece in pieces:
        value = piece[...].astype(F32)
        square = jnp.sum(value * value, axis=1, keepdims=True)
        total = square if total is None else total + square
    scale = lax.rsqrt(total / (4 * HD) + EPS)
    for piece, place in zip(pieces, heads):
        columns = pl.ds(pl.multiple_of(place * HD, HD), HD)
        out_ref[0, :, columns] = (piece[...].astype(F32) * scale * gain_ref[0:1, columns]).astype(BF)


def normalise(ids, group, groups, pieces, gain, former):
    tokens = pieces[0].shape[0]
    part = pl.BlockSpec((tokens, HD), lambda i, ids: (0, 0))
    more = [] if former is None else [former]
    return pl.pallas_call(
        norm_kernel,
        out_shape=jax.ShapeDtypeStruct((groups, tokens, 4 * HD), BF),
        grid_spec=pltpu.PrefetchScalarGridSpec(
            num_scalar_prefetch=1,
            grid=(1,),
            in_specs=[part] * 4
            + [pl.BlockSpec((1, 4 * HD), lambda i, ids: (0, 0))]
            + [pl.BlockSpec(memory_space=pl.ANY)] * len(more),
            out_specs=pl.BlockSpec((1, tokens, 4 * HD), lambda i, ids: (group, 0, 0)),
        ),
        input_output_aliases={} if former is None else {6: 0},
        compiler_params=params(),
        cost_estimate=cost(8 * tokens * HD * 4, 4 * tokens * HD * 4),
    )(ids, *pieces, gain, *more)


SWAP = [(0, 1), (1, 0)]
BOTH = [(0, 3), (1, 2), (2, 1), (3, 0)]


def body(inputs, projections, lrate, fast_init, gain):
    groups = inputs.shape[0]
    plane = lax.axis_index("z_hi").astype(jnp.int32)
    core = lax.axis_index("core").astype(jnp.int32)
    far = lax.axis_index("head").astype(jnp.int32)
    kept = jnp.stack([plane, far])
    given = jnp.stack([1 - plane, far])
    share = jnp.stack([plane, core])
    gain = gain.reshape(1, -1)
    rates = lrate.transpose(0, 2, 1)

    def across(x):
        return lax.ppermute(x, "core", SWAP)

    def beyond(x):
        return lax.ppermute(x, "z_hi", SWAP)

    def after(ids, dep):
        return ids if dep is None else lax.optimization_barrier((ids, dep))[0]

    def of(ids, jobs, dep=None):
        return project(after(ids, dep), jobs, inputs, projections, rates)

    def forward(far_parts):
        return (
            lax.ppermute(far_parts[0], "head", SWAP),
            lax.ppermute(far_parts[1], ("z_hi", "head"), BOTH),
        )

    def to_rows(far_parts, near_parts):
        return near_parts[0], beyond(near_parts[1]), *forward(far_parts)

    def summed(grads, beside_sum=None, beside_gather=None):
        parts, first = exchange(grads, beside_sum)
        shard, squares = sum_shards(parts)
        shards, second = exchange(with_notes(shard, squares, across(squares)), beside_gather)
        return shards, first, second

    def readouts(memory, *asked):
        mate = across(memory)
        return read(1, memory, mate, *asked), read(0, memory, mate, *asked)

    later = ((1, 1), (1, 2), (1, 0), (0, 0))
    (given_now,) = of(given, ((0, 1), (0, 2)))
    foreign = beyond(given_now)
    (own,) = of(kept, ((0, 1), (0, 2)))
    own_mate = across(own)
    given_next, given_asked = of(given, later, own)
    memory, target = start_memory(after(share, given_next), fast_init)
    foreign, memory, given_next, given_asked = lax.optimization_barrier((foreign, memory, given_next, given_asked))
    foreign_next = beyond(given_next)
    foreign_asked = beyond(given_asked)
    pieces = (own, own_mate, foreign, across(foreign))
    grads = first_step(memory, pieces)
    shards, (own_next, own_asked), _ = summed(grads, lambda dep: tuple(of(kept, later, dep)))
    grads, memory = next_step(memory, shards, target, pieces)
    shards, (foreign_next, foreign_asked, own_next_mate), foreign_next_mate = summed(
        grads,
        lambda dep: (foreign_next, foreign_asked, across(own_next)),
        lambda dep: across(foreign_next),
    )
    pieces = (own_next, own_next_mate, foreign_next, foreign_next_mate)

    grads, memory = next_step(memory, shards, target, pieces)
    then, mate = memory, across(memory)
    parts, first = exchange(grads, lambda dep: mate)
    shard, squares = sum_shards(parts)
    asked = (own_asked, 1, foreign_asked, 1)
    far_parts, near_parts = read(1, then, first, *asked), read(0, then, first, *asked)
    message = with_notes(shard, squares, across(squares))
    message, far_parts, near_parts = lax.optimization_barrier((message, far_parts, near_parts))
    shards, _ = exchange(message, None)
    ahead, askew = forward(far_parts)
    beside = beyond(near_parts[1])
    grads, memory = next_step(memory, shards, target, pieces)
    shards, beside, (ahead, askew) = summed(grads, lambda dep: beside, lambda dep: (ahead, askew))
    rows_then = (near_parts[0], beside, ahead, askew)
    memory = last_memory(memory, shards, target)
    rows = to_rows(*readouts(memory, own_asked, 0, foreign_asked, 0))
    result = normalise(after(kept, memory), 0, groups, rows_then, gain, None)
    return normalise(kept, 1, groups, rows, gain, result)


def solution(mesh):
    finer = Mesh(
        mesh.devices.reshape(4, 2, 4, 2, mesh.shape["head"]),
        (*TOK, "head"),
    )
    placed = (
        P(None, TOK, None),
        P(None, None, "head"),
        P(None, TOK, "head"),
        P("head", None, None, None),
        P(),
    )
    return jax.shard_map(
        body, mesh=finer, in_specs=placed, out_specs=P(None, (*TOK, "head"), None), check_vma=False
    )
```
